32 devices in a mesh: ctx: 4 (over x, core), wide: 8 (over z, y).
Axes of the slice: x: 2, y: 2, z: 4, core: 2. Of those that a mesh axis runs over, the one named last changes fastest.
Arguments:
- tokens: bfloat16 [4096, 2688], P(('ctx', 'wide')), may hold values from -10 to 10
- mamba_gain: float32 [2688], replicated, may hold values from 0.25 to 1.75
- w_z: bfloat16 [2688, 4096], P(None, 'wide'), may hold values from -0.125 to 0.125
- w_x: bfloat16 [2688, 4096], P(None, 'wide'), may hold values from -0.125 to 0.125
- w_bc: bfloat16 [2688, 2048], P(None, 'wide'), may hold values from -0.125 to 0.125
- w_dt: bfloat16 [2688, 64], replicated, may hold values from -1 to 1
- dt_bias: float32 [64], P('wide'), may hold values from -2 to 0
- a_log: float32 [64], P('wide')
- conv_x: float32 [4, 4096], P(None, 'wide'), may hold values from -3 to 3
- conv_bc: float32 [4, 2048], replicated, may hold values from -3 to 3
- skip: float32 [64], P('wide'), may hold values from 0.5 to 1.5
- norm_gain: float32 [4096], P('wide'), may hold values from 0.25 to 1.75
- w_out: bfloat16 [4096, 2688], P('wide'), may hold values from -0.09375 to 0.09375
- moe_gain: float32 [2688], replicated, may hold values from 0.25 to 1.75
- expert_ids: int32 [4096, 6], P(('ctx', 'wide')), may hold values from 0 to 31, all different within a row; in each aligned block of 128 rows (0 to 127, 128 to 255, ...) at most 28 rows name the same one
- router_weights: float32 [4096, 6], P(('ctx', 'wide')), may hold values from 0.05 to 0.5
- w_up: bfloat16 [32, 2688, 1856], P(('ctx', 'wide')), may hold values from -0.125 to 0.125
- w_down: bfloat16 [32, 1856, 2688], P(('ctx', 'wide')), may hold values from -0.125 to 0.125
Outputs:
- mixed: bfloat16 [4096, 2688], P(('ctx', 'wide'))
The draws below stay inside these ranges and needn't reach their ends.
Inputs may be any that keep to these rules, and one draw needn't show every extreme that they name: `expert_ids`: within the rows of one device (128 tokens), no expert is named more than 28 times, and a row names 6 different experts.
All inputs are finite; a program needn't handle non-finite values.
Results may differ from the reference program's by a relative error of at most 0.015.
Values may be sent and summed in bfloat16 or wider, within the bound.
No kernel may reach another device: no remote copies, remote signals or barrier semaphores. Data moves between devices by JAX's collectives and lax.ppermute only.
A program may use at most 128 MiB of HBM per device.

```python
import math
import jax
import jax.numpy as jnp
import numpy as np
from jax import lax

D = 2688
HEADS = 64
HEAD_DIM = 64
STATE = 128
GROUPS = 8
KERNEL = 4
FFE = 1856
TOP = 6
BLOCK = 128
TOK_DEV = 128
INNER = 4096
SPAN = 1024
LENGTH = 4096
EXPERTS = 32
CAP = 28
N_CTX = 4
N_WIDE = 8


def shared_direction(key):
    return jax.random.normal(jax.random.fold_in(key, 501), (D,), jnp.float32)


def draw_tokens(key, part):
    direction = shared_direction(key)
    key_noise, key_level = jax.random.split(jax.random.fold_in(key, 23), 2)
    regions = LENGTH // (SPAN // 2)
    levels = jax.random.uniform(key_level, (regions,), jnp.float32, 0.0, 1.5)
    per_row = jnp.repeat(levels, SPAN // 2)
    noise = jax.random.normal(key_noise, (LENGTH, D), jnp.float32)
    values = noise + per_row[:, None] * direction[None, :]
    return jnp.clip(values, -10.0, 10.0).astype(jnp.bfloat16)


def draw_w_dt(key, part):
    direction = shared_direction(key)
    key_noise, key_strength = jax.random.split(jax.random.fold_in(key, 37), 2)
    noise = jax.random.normal(key_noise, (D, HEADS), jnp.float32) / jnp.sqrt(jnp.float32(D))
    strength = jax.random.uniform(key_strength, (HEADS,), jnp.float32, 2.0, 4.0)
    values = noise + direction[:, None] * strength[None, :] / D
    return jnp.clip(values, -1.0, 1.0).astype(jnp.bfloat16)


def draw_a_log(key, part):
    key_slow, key_fast, key_order = jax.random.split(jax.random.fold_in(key, 11), 3)
    slow_rates = jnp.log(jax.random.uniform(key_slow, (HEADS,), jnp.float32, 0.7, 1.5) / LENGTH)
    fast_rates = jax.random.uniform(key_fast, (HEADS,), jnp.float32, jnp.log(0.05), jnp.log(0.2))
    rank_order = jax.random.permutation(key_order, HEADS)
    keep_state = rank_order >= HEADS // 2
    return jnp.where(keep_state, slow_rates, fast_rates)


def block_levels(stream_key, extent, shards, smallest, high):
    factor_of = 1.0
    for position, shards_of in shards:
        steps = jax.random.uniform(jax.random.fold_in(jax.random.fold_in(stream_key, 6), position), (shards_of,), jnp.float32, smallest / len(shards), high / len(shards))
        factor_of = factor_of * jnp.repeat(jnp.exp(steps), extent[position] // shards_of).reshape((-1,) + (1,) * (len(extent) - 1 - position))
    return factor_of


def deal_out(key, own, number, rows, count, top, most, skew):
    order = jax.random.permutation(key, count)
    crowded, ordinary = load_shares(count, rows * top, most, skew, True), load_shares(count, rows * top, most, skew, False)
    places = jnp.arange(count)

    def named(sizes, rotation):
        used = int((sizes > 0).sum())
        fixed = max(1, used // 4)
        passed = fixed + (places - fixed + rotation * (used - fixed)) % max(1, count - fixed)
        return jnp.zeros((count,), jnp.int32).at[order[jnp.where(places < fixed, places, passed)]].set(jnp.asarray(sizes, jnp.int32))

    sizes = jnp.where(number % 4 == 0, named(crowded, number // 4), named(ordinary, number - number // 4 - 1))
    mixed = jax.random.permutation(jax.random.fold_in(own, 3), count)
    giver, sink = mixed[0:count // 2 * 2:2], mixed[1:count // 2 * 2:2]
    slack = jnp.minimum(sizes[giver] - 1, most - sizes[sink]) // 2
    slack = jnp.where((giver == order[0]) | (sink == order[0]) | (sizes[sink] == 0), 0, jnp.maximum(slack, 0))
    passed = jax.random.randint(jax.random.fold_in(own, 4), (count // 2,), 0, 1 << 20) % (slack + 1)
    sizes = sizes.at[giver].add(-passed).at[sink].add(passed)
    labels = jnp.searchsorted(jnp.cumsum(sizes), jnp.arange(rows * top), side="right").astype(jnp.int32)
    listing = labels.reshape(top, rows).T
    listing = listing[jax.random.permutation(jax.random.fold_in(own, 1), rows)]
    rotation = jax.random.randint(jax.random.fold_in(own, 2), (rows, 1), 0, top)
    return jnp.take_along_axis(listing, (jnp.arange(top)[None, :] + rotation) % top, axis=1)


def load_shares(count, total, limit, lean, full):
    loads = [(1 << 20) // math.isqrt(grade ** lean) + 1 for grade in range(1, count + 1)]
    largest = limit if full else min(limit, max(-(-total // count), total * loads[0] // sum(loads)))
    least = 1 if total - largest >= count - 1 else 0
    counts, surplus = [largest] + [least] * (count - 1), total - largest - least * (count - 1)
    while surplus > 0:
        candidates = [i for i in range(1, count) if counts[i] < largest] or [i for i in range(1, count) if counts[i] < limit]
        pool, remaining = sum([loads[i] for i in candidates]), surplus
        for i in candidates:
            more = min(limit - counts[i], max(1, remaining * loads[i] // pool), surplus)
            counts[i] = counts[i] + more
            surplus = surplus - more
    return np.array(counts)


def gaussian(key, extent, width, limit, cuts=(), kind=jnp.bfloat16):
    result = width * jax.random.normal(key, extent, jnp.float32)
    if cuts:
        result = result * block_levels(key, extent, cuts, -0.22, 0.18)
    return jnp.clip(result, -limit, limit).astype(kind)


def setup_inputs(seed: int = 0) -> dict:
    key_list = jax.random.split(jax.random.key(seed), 19)
    tokens = draw_tokens(jax.random.fold_in(key_list[18], 71), 0)
    mamba_gain = jnp.clip(1.0 + 0.15 * jax.random.normal(key_list[1], (D,), jnp.float32), 0.25, 1.75)
    w_z = gaussian(key_list[2], (D, INNER), D ** -0.5, 0.125, ((1, 8),))
    w_x = gaussian(key_list[3], (D, INNER), D ** -0.5, 0.125, ((1, 8),))
    w_bc = gaussian(key_list[4], (D, 2 * GROUPS * STATE), D ** -0.5, 0.125, ((1, 8),))
    w_dt = draw_w_dt(jax.random.fold_in(key_list[18], 71), 0)
    dt_bias = jnp.clip(-2.0 + 2.0 * jax.random.uniform(key_list[6], (HEADS,), jnp.float32) ** block_levels(key_list[6], (HEADS,), ((0, 8),), -0.2, 0.2), -2.0, 0.0)
    a_log = draw_a_log(jax.random.fold_in(key_list[18], 71), 0)
    conv_x = gaussian(key_list[8], (KERNEL, INNER), 0.5, 3.0, ((1, 8),), jnp.float32)
    conv_bc = gaussian(key_list[9], (KERNEL, 2 * GROUPS * STATE), 0.5, 3.0, (), jnp.float32)
    skip = jnp.clip(0.5 + 1.0 * jax.random.uniform(key_list[10], (HEADS,), jnp.float32) ** block_levels(key_list[10], (HEADS,), ((0, 8),), -0.2, 0.2), 0.5, 1.5)
    norm_gain = jnp.clip(1.0 + 0.15 * jax.random.normal(key_list[11], (INNER,), jnp.float32), 0.25, 1.75)
    w_out = gaussian(key_list[12], (INNER, D), INNER ** -0.5, 0.09375, ((0, 8),))
    moe_gain = jnp.clip(1.0 + 0.15 * jax.random.normal(key_list[13], (D,), jnp.float32), 0.25, 1.75)
    expert_ids_keys = jax.random.split(jax.random.fold_in(key_list[14], 1), LENGTH // TOK_DEV)
    expert_ids_turns = jax.random.permutation(jax.random.fold_in(key_list[14], 3), LENGTH // TOK_DEV)
    expert_ids = jax.vmap(lambda own, number: deal_out(jax.random.fold_in(key_list[14], 2), own, number, TOK_DEV, EXPERTS, TOP, CAP, 2))(expert_ids_keys, expert_ids_turns).reshape((LENGTH, TOP))
    router_weights = jnp.clip(jnp.exp(math.log(0.5) - 2.3025851 * jax.random.uniform(key_list[15], (LENGTH, TOP), jnp.float32) ** block_levels(key_list[15], (LENGTH, TOP), ((0, 32),), -0.2, 0.2)), 0.05, 0.5)
    w_up = gaussian(key_list[16], (EXPERTS, D, FFE), D ** -0.5, 0.125, ((0, 32),))
    w_down = gaussian(key_list[17], (EXPERTS, FFE, D), FFE ** -0.5, 0.125, ((0, 32),))
    return dict(tokens=tokens, mamba_gain=mamba_gain, w_z=w_z, w_x=w_x, w_bc=w_bc, w_dt=w_dt, dt_bias=dt_bias, a_log=a_log, conv_x=conv_x, conv_bc=conv_bc, skip=skip, norm_gain=norm_gain, w_out=w_out, moe_gain=moe_gain, expert_ids=expert_ids, router_weights=router_weights, w_up=w_up, w_down=w_down)


EPSILON = 1e-05
PRECISE = lax.Precision.HIGHEST

def rms_scale(values, gain_vec):
    mean_sq = lax.optimization_barrier(jnp.mean(values * values, axis=-1, keepdims=True))
    return values * lax.rsqrt(mean_sq + EPSILON) * gain_vec

def causal_conv(pre_conv, taps):
    length = pre_conv.shape[0]
    padded = jnp.concatenate([jnp.zeros((KERNEL - 1, pre_conv.shape[1]), jnp.float32), pre_conv.astype(jnp.float32)], 0)
    total = jnp.zeros(pre_conv.shape, jnp.float32)
    for offset in range(KERNEL):
        total = total + taps[offset] * padded[offset:offset + length]
    return jax.nn.silu(total)

def slot_numbers(flat_ids):
    onehot = (flat_ids[:, None] == jnp.arange(EXPERTS, dtype=jnp.int32)[None, :]).astype(jnp.int32)
    before = jnp.cumsum(onehot, axis=0) - onehot
    return lax.optimization_barrier(jnp.sum(before * onehot, axis=1))

def ssd_block(carried, inputs):
    x_blocks, b_blocks, c_blocks, log_decay, step_size = inputs
    cum_decay = jnp.cumsum(log_decay, axis=0)
    per_group = HEADS // GROUPS
    scores = jnp.einsum('igs,jgs->gij', c_blocks, b_blocks, precision=PRECISE)
    scores = jnp.repeat(scores, per_group, axis=0)
    cum_heads = cum_decay.T
    gap_decay = cum_heads[:, :, None] - cum_heads[:, None, :]
    causal = jnp.arange(BLOCK)[:, None] >= jnp.arange(BLOCK)[None, :]
    decay_mask = jnp.exp(jnp.where(causal[None], gap_decay, -jnp.inf))
    weights = scores * decay_mask * step_size.T[:, None, :]
    y_intra = jnp.einsum('hij,jhp->ihp', weights, x_blocks, precision=PRECISE)
    c_heads = jnp.repeat(c_blocks, per_group, axis=1)
    b_heads = jnp.repeat(b_blocks, per_group, axis=1)
    y_inter = jnp.exp(cum_decay)[:, :, None] * jnp.einsum('ihs,hps->ihp', c_heads, carried, precision=PRECISE)
    tail_factor = jnp.exp(cum_decay[-1][None, :] - cum_decay) * step_size
    updated = jnp.exp(cum_decay[-1])[:, None, None] * carried + jnp.einsum('jh,jhp,jhs->hps', tail_factor, x_blocks, b_heads, precision=PRECISE)
    return (updated, y_intra + y_inter)

def reference(tokens, mamba_gain, w_z, w_x, w_bc, w_dt, dt_bias, a_log, conv_x, conv_bc, skip, norm_gain, w_out, moe_gain, expert_ids, router_weights, w_up, w_down):
    stream = tokens.astype(jnp.float32)
    normed = rms_scale(stream, mamba_gain).astype(jnp.bfloat16)
    gate_in = jnp.dot(normed, w_z, preferred_element_type=jnp.float32).astype(jnp.bfloat16)
    x_in = jnp.dot(normed, w_x, preferred_element_type=jnp.float32).astype(jnp.bfloat16)
    bc_in = jnp.dot(normed, w_bc, preferred_element_type=jnp.float32).astype(jnp.bfloat16)
    step_size = jax.nn.softplus(jnp.dot(normed, w_dt, preferred_element_type=jnp.float32) + dt_bias)
    log_decay = -jnp.exp(a_log) * step_size
    x_conv = causal_conv(x_in, conv_x)
    bc_conv = causal_conv(bc_in, conv_bc).reshape(LENGTH, GROUPS, 2, STATE)
    blocks = LENGTH // BLOCK
    x_blocks = x_conv.reshape(blocks, BLOCK, HEADS, HEAD_DIM)
    b_blocks = bc_conv[:, :, 0].reshape(blocks, BLOCK, GROUPS, STATE)
    c_blocks = bc_conv[:, :, 1].reshape(blocks, BLOCK, GROUPS, STATE)
    start_state = jnp.zeros((HEADS, HEAD_DIM, STATE), jnp.float32)
    _, y_total = lax.scan(ssd_block, start_state, (x_blocks, b_blocks, c_blocks, log_decay.reshape(blocks, BLOCK, HEADS), step_size.reshape(blocks, BLOCK, HEADS)))
    x_heads = x_conv.reshape(LENGTH, HEADS, HEAD_DIM)
    y_total = y_total.reshape(LENGTH, HEADS, HEAD_DIM) + skip[:, None] * x_heads
    gated = y_total * jax.nn.silu(gate_in.astype(jnp.float32)).reshape(LENGTH, HEADS, HEAD_DIM)
    gated = gated * lax.rsqrt(lax.optimization_barrier(jnp.mean(gated * gated, axis=-1, keepdims=True)) + EPSILON)
    gated = (gated.reshape(LENGTH, INNER) * norm_gain).astype(jnp.bfloat16)
    share_width = INNER // N_WIDE

    def add_share(total, wide_index):
        gated_part = lax.dynamic_slice_in_dim(gated, wide_index * share_width, share_width, 1)
        weight_part = lax.dynamic_slice_in_dim(w_out, wide_index * share_width, share_width, 0)
        partial_sum = jnp.dot(gated_part, weight_part, preferred_element_type=jnp.float32).astype(jnp.bfloat16)
        partial_sum = lax.optimization_barrier(partial_sum)
        return (total + partial_sum.astype(jnp.float32), None)
    mamba_out, _ = lax.scan(add_share, jnp.zeros((LENGTH, D), jnp.float32), jnp.arange(N_WIDE, dtype=jnp.int32))
    hidden_stream = (stream + mamba_out).astype(jnp.bfloat16)
    hidden_f32 = hidden_stream.astype(jnp.float32)
    moe_in = rms_scale(hidden_f32, moe_gain).astype(jnp.bfloat16)
    devices = N_CTX * N_WIDE
    flat_ids = expert_ids.reshape(devices, TOK_DEV * TOP)
    slots = jax.vmap(slot_numbers)(flat_ids)
    source = jnp.arange(devices, dtype=jnp.int32)[:, None]
    row_index = jnp.arange(TOK_DEV * TOP, dtype=jnp.int32)[None, :]
    token_index = source * TOK_DEV + row_index // TOP
    slot_index = flat_ids * (devices * CAP) + source * CAP + slots
    slot_table = jnp.full((EXPERTS * devices * CAP,), LENGTH, jnp.int32).at[slot_index.reshape(-1)].set(token_index.reshape(-1))
    slot_weight = jnp.zeros((EXPERTS * devices * CAP,), jnp.float32).at[slot_index.reshape(-1)].set(router_weights.reshape(-1))
    padded_in = jnp.concatenate([moe_in, jnp.zeros((1, D), jnp.bfloat16)], 0)

    def run_expert(accumulated, expert_index):
        slot_rows = lax.dynamic_slice_in_dim(slot_table, expert_index * devices * CAP, devices * CAP, 0)
        row_weight = lax.dynamic_slice_in_dim(slot_weight, expert_index * devices * CAP, devices * CAP, 0)
        picked_rows = padded_in[slot_rows]
        up_proj = jnp.dot(picked_rows, w_up[expert_index], preferred_element_type=jnp.float32)
        activated = jax.nn.relu(up_proj)
        activated = (activated * activated).astype(jnp.bfloat16)
        expert_out = jnp.dot(activated, w_down[expert_index], preferred_element_type=jnp.float32).astype(jnp.bfloat16)
        contrib = expert_out.astype(jnp.float32) * row_weight[:, None]
        return (accumulated.at[slot_rows].add(contrib), None)
    accumulated, _ = lax.scan(run_expert, jnp.zeros((LENGTH + 1, D), jnp.float32), jnp.arange(EXPERTS, dtype=jnp.int32))
    return (hidden_f32 + accumulated[:LENGTH]).astype(jnp.bfloat16)
```

```python
import functools

import jax
import jax.numpy as jnp
from jax import lax
from jax.experimental import pallas as pl
from jax.experimental.pallas import tpu as pltpu
from jax.sharding import PartitionSpec as P

STATE = 128
GROUPS = 8
KERNEL = 4
TOP = 6
RIM = 8

EPSILON = 1e-05
PRECISE = lax.Precision.HIGHEST
VMEM_BYTES = 48 * 1024 * 1024


def ring_of(count):
    columns = 1
    while columns * columns * 4 <= count:
        columns *= 2
    rows = count // columns
    if columns == 1 or rows % 2:
        return list(range(count))
    walk = [row * columns for row in range(rows)]
    for lap, row in enumerate(reversed(range(rows))):
        line = list(range(1, columns))
        if lap % 2:
            line.reverse()
        walk += [row * columns + column for column in line]
    return walk


class Ring:
    def __init__(self, count):
        self.count = count
        self.half = count // 2
        self.walk = ring_of(count)
        place = [0] * count
        for spot, index in enumerate(self.walk):
            place[index] = spot
        following = [(self.walk[i], self.walk[(i + 1) % count]) for i in range(count)]
        self.routes = {1: following, -1: [(b, a) for a, b in following]}
        here = jnp.asarray(place, jnp.int32)[lax.axis_index("wide")]
        self.groups = [[0]] + [[s, -s] for s in range(1, self.half)] + [[self.half]]
        flat = jnp.asarray([o for group in self.groups for o in group], jnp.int32)
        self.order = jnp.asarray(self.walk, jnp.int32)[(here + flat + count) % count]

    def send(self, block, way):
        return lax.ppermute(block, "wide", self.routes[way])

    def gather(self, block):
        yield block
        ahead = behind = block
        for _ in range(1, self.half):
            behind = self.send(behind, 1)
            ahead = self.send(ahead, -1)
            yield jnp.concatenate([ahead, behind], 0)
        cut = block.shape[0] // 2
        yield jnp.concatenate([self.send(behind[:cut], 1), self.send(ahead[cut:], -1)], 0)

    def scatter_sum(self, parts):
        rows = parts[0].shape[0]
        cut = rows // 2
        far = parts[self.half]
        up, down = self.send(far[:cut], 1), self.send(far[cut:], -1)
        for s in range(self.half - 1, 0, -1):
            ahead, behind = parts[s][:rows], parts[s][rows:]
            if s == self.half - 1:
                none = jnp.zeros_like(up)
                up = jnp.concatenate([up, none], 0)
                down = jnp.concatenate([none, down], 0)
            up = self.send((ahead.astype(jnp.float32) + up.astype(jnp.float32)).astype(far.dtype), 1)
            down = self.send((behind.astype(jnp.float32) + down.astype(jnp.float32)).astype(far.dtype), -1)
        return parts[0].astype(jnp.float32) + up.astype(jnp.float32) + down.astype(jnp.float32)


def partner_2(block, axis, bit):
    count = lax.axis_size(axis)
    route = []
    for low in range(count):
        high = low | 1 << bit
        if high != low and high < count:
            route += [(low, high), (high, low)]
    return lax.ppermute(block, axis, route)


def shifted(block, axis, distance):
    devices = range(lax.axis_size(axis))
    route = [(i - distance, i) for i in devices if i - distance in devices]
    return lax.ppermute(block, axis, route)


def doubled_gather(block, axis):
    index = lax.axis_index(axis)
    for bit_number in range(lax.axis_size(axis).bit_length() - 1):
        other = partner_2(block, axis, bit_number)
        upper = index // 2**bit_number % 2 == 1
        block = jnp.where(
            upper, jnp.concatenate([other, block], 0), jnp.concatenate([block, other], 0)
        )
    return block


def last_of(block, axis):
    index = lax.axis_index(axis)
    for bit_number in range(lax.axis_size(axis).bit_length() - 1):
        other = partner_2(block, axis, bit_number)
        block = jnp.where(index // 2**bit_number % 2 == 1, block, other)
    return block


def rms_scale(values, gain_vec):
    mean_sq = jnp.mean(values * values, axis=-1, keepdims=True)
    return values * lax.rsqrt(mean_sq + EPSILON) * gain_vec


def spread(values, fan):
    high = values.astype(jnp.bfloat16)
    low = (values - high.astype(jnp.float32)).astype(jnp.bfloat16)
    return jnp.dot(high, fan, preferred_element_type=jnp.float32) + jnp.dot(
        low, fan, preferred_element_type=jnp.float32
    )


def softplus(values):
    return jnp.maximum(values, 0.0) + jnp.log1p(jnp.exp(-jnp.abs(values)))


def silu(values):
    return values / (1.0 + jnp.exp(-values))


def conv_silu(current, before, taps):
    rows = current.shape[0]
    extended = jnp.concatenate([before, current], 0)
    first = RIM - (KERNEL - 1)
    total = taps[0:1] * extended[first : first + rows]
    for offset in range(1, KERNEL):
        total = total + taps[offset : offset + 1] * extended[first + offset : first + offset + rows]
    return silu(total)


def ssd_kernel(groups, refs):
    count = sum(groups)
    order = refs[0]
    pieces = len(groups)
    x_in, bc_in, dt_in, dtt_in = (refs[1 + k * pieces : 1 + (k + 1) * pieces] for k in range(4))
    (
        rim_x, rim_bc, bias_row, bias_col, rate_row, rate_col, taps_x, taps_bc, skip_row, fan,
        y_out, c_out, cum_out, state_out,
        xs, bcs, dts, dtts, before_x, before_bc, state, passed, arrivals,
    ) = refs[1 + 4 * pieces :]
    rows = xs.shape[1]
    heads = bias_row.shape[1]
    width = xs.shape[2]
    head_dim = width // heads
    copies = []
    spot = 0
    for g, size in enumerate(groups):
        for j in range(size):
            seq = order[spot]
            span = pl.ds(j * rows, rows)
            moves = [
                (x_in[g].at[span], xs.at[seq]),
                (bc_in[g].at[span], bcs.at[seq]),
                (dt_in[g].at[span], dts.at[seq]),
                (dtt_in[g].at[:, span], dtts.at[seq]),
            ]
            for k, (source, target) in enumerate(moves):
                copies.append(pltpu.make_async_copy(source, target, arrivals.at[k, spot]))
                copies[-1].start()
            spot += 1
    for copy in copies:
        copy.wait()
    before_x[...] = rim_x[...].astype(jnp.float32)
    before_bc[...] = rim_bc[...].astype(jnp.float32)
    state[...] = jnp.zeros_like(state)
    passed[...] = jnp.zeros_like(passed)
    row_id = lax.broadcasted_iota(jnp.int32, (rows, rows), 0)
    col_id = lax.broadcasted_iota(jnp.int32, (rows, rows), 1)
    causal = row_id >= col_id
    lower = jnp.where(causal, 1.0, 0.0).astype(jnp.float32)
    upper = jnp.where(row_id <= col_id, 1.0, 0.0).astype(jnp.float32)
    pair = 2 * head_dim
    left = lax.broadcasted_iota(jnp.int32, (rows, pair), 1) < head_dim

    def one(i, carry):
        x_now = xs[i].astype(jnp.float32)
        bc_now = bcs[i].astype(jnp.float32)
        x = conv_silu(x_now, before_x[...], taps_x[...])
        bc = conv_silu(bc_now, before_bc[...], taps_bc[...])
        before_x[...] = x_now[rows - RIM :]
        before_bc[...] = bc_now[rows - RIM :]
        b = bc[:, :STATE]
        c = bc[:, STATE:].astype(jnp.bfloat16)
        b_t = jnp.transpose(b).astype(jnp.bfloat16)
        dt = softplus(dts[i] + bias_row[...])
        dt_t = softplus(dtts[i] + bias_col[...])
        cum = jnp.dot(lower, dt * rate_row[...], precision=PRECISE, preferred_element_type=jnp.float32)
        cum_t = jnp.dot(dt_t * rate_col[...], upper, precision=PRECISE, preferred_element_type=jnp.float32)
        last = cum[rows - 1 : rows]
        scores = jnp.dot(c, b_t, preferred_element_type=jnp.float32)
        x_dt = x * spread(dt, fan[...])
        x_low = x_dt.astype(jnp.bfloat16)
        earlier = jnp.dot(c, state[...].astype(jnp.bfloat16), preferred_element_type=jnp.float32)
        rest = spread(jnp.exp(cum), fan[...]) * earlier + skip_row[...] * x
        for h in range(0, heads, 2):
            weights = []
            for k in (h, h + 1):
                gap = cum[:, k : k + 1] - cum_t[k : k + 1, :]
                weights.append((scores * jnp.exp(jnp.where(causal, gap, -1e30))).astype(jnp.bfloat16))
            units = slice(h * head_dim, h * head_dim + pair)
            both = x_low[:, units]
            none = jnp.zeros_like(both)
            stacked = jnp.concatenate([jnp.where(left, both, none), jnp.where(left, none, both)], 0)
            y = jnp.dot(jnp.concatenate(weights, 1), stacked, preferred_element_type=jnp.float32)
            y_out[i, :, units] = y + rest[:, units]
        tail = (x_dt * spread(jnp.exp(last - cum), fan[...])).astype(jnp.bfloat16)
        grown = jnp.dot(b_t, tail, preferred_element_type=jnp.float32)
        c_out[i] = c
        cum_out[i] = cum + passed[...]
        passed[...] = passed[...] + last
        fade = spread(jnp.broadcast_to(jnp.exp(last), (8, heads)), fan[...])
        state[...] = fade[0:1] * state[...] + grown
        return carry

    lax.fori_loop(0, count, one, 0)
    state_out[:STATE] = state[...]
    state_out[STATE:] = spread(jnp.broadcast_to(passed[...], (8, heads)), fan[...])


def gate_kernel(groups, refs):
    order, y_in, c_in, cum_in, state_in, gain_row, fan, gather = refs[:8]
    gates = refs[8 : 8 + len(groups)]
    outs = refs[8 + len(groups) :]
    rows = y_in.shape[1]
    head_dim = y_in.shape[2] // cum_in.shape[2]
    incoming = state_in[...].astype(jnp.bfloat16)
    spot = 0
    for g, size in enumerate(groups):
        for j in range(size):
            seq = order[spot]
            span = slice(j * rows, (j + 1) * rows)
            earlier = jnp.dot(c_in[seq], incoming, preferred_element_type=jnp.float32)
            y = y_in[seq] + spread(jnp.exp(cum_in[seq]), fan[...]) * earlier
            gated = y * silu(gates[g][span].astype(jnp.float32))
            squares = jnp.dot(
                (gated * gated).astype(jnp.bfloat16), gather[...], preferred_element_type=jnp.float32
            )
            scale = lax.rsqrt(squares / head_dim + EPSILON)
            outs[g][span] = (gated * spread(scale, fan[...]) * gain_row[...]).astype(jnp.bfloat16)
            spot += 1


def vmem(count):
    return [pl.BlockSpec(memory_space=pltpu.VMEM)] * count


def call(kernel, ins, outs, scratch, flops, far=0):
    moved = sum(a.size * a.dtype.itemsize for a in list(ins) + list(outs))
    return pl.pallas_call(
        lambda *refs: kernel(refs),
        out_shape=outs,
        in_specs=[pl.BlockSpec(memory_space=pltpu.SMEM)]
        + [pl.BlockSpec(memory_space=pl.ANY)] * far
        + vmem(len(ins) - 1 - far),
        out_specs=vmem(len(outs)),
        scratch_shapes=scratch,
        compiler_params=pltpu.CompilerParams(vmem_limit_bytes=VMEM_BYTES),
        cost_estimate=pl.CostEstimate(flops=flops, bytes_accessed=moved, transcendentals=0),
    )(*ins)


def shards(
    tokens,
    mamba_gain,
    w_z,
    w_x,
    w_bc,
    w_dt,
    dt_bias,
    a_log,
    conv_x,
    conv_bc,
    skip,
    norm_gain,
    w_out,
    moe_gain,
    expert_ids,
    router_weights,
    w_up,
    w_down,
):
    wide_count = lax.axis_size("wide")
    ctx_count = lax.axis_size("ctx")
    tok_rows, model_width = tokens.shape
    heads_here = dt_bias.shape[0]
    inner_here = w_z.shape[1]
    head_dim = inner_here // heads_here
    position = lax.axis_index("wide")
    ctx_index = lax.axis_index("ctx")
    ring = Ring(wide_count)
    sizes = [len(group) for group in ring.groups]
    bf16, f32 = jnp.bfloat16, jnp.float32

    stream = tokens.astype(f32)
    normed = rms_scale(stream, mamba_gain).astype(bf16)

    choices = jnp.concatenate([expert_ids.astype(f32), router_weights], 1)
    span_choices = doubled_gather(choices, "wide").reshape(wide_count, tok_rows, 2 * TOP)[ring.order]
    experts = ctx_count * wide_count
    capacity = max(2, (7 * tok_rows * TOP + 6 * experts - 1) // (6 * experts))
    peers = (ctx_index ^ jnp.arange(ctx_count, dtype=jnp.int32)) * wide_count + position
    picks, weighings = [], []
    start = 0
    for size in sizes:
        part = span_choices[start : start + size].reshape(size * tok_rows, 2 * TOP)
        start += size
        chosen = part[:, :TOP].astype(jnp.int32)
        named = chosen[None] == peers[:, None, None]
        member = jnp.any(named, axis=2)
        weight = jnp.sum(jnp.where(named, part[None, :, TOP:], 0.0), axis=2)
        counted = member.astype(jnp.int32)
        rank = jnp.cumsum(counted, axis=1) - counted
        slots = jnp.arange(size * capacity, dtype=jnp.int32)
        here = member[:, None, :] & (rank[:, None, :] == slots[None, :, None])
        picks.append(here.astype(bf16).reshape(-1, size * tok_rows))
        weighings.append(
            jnp.where(here, weight[:, None, :], 0.0).astype(bf16).reshape(-1, size * tok_rows)
        )

    w_steps = lax.dynamic_slice_in_dim(w_dt, position * heads_here, heads_here, 1)
    members = wide_count // GROUPS

    def whole_bc(share):
        for bit_number in range(members.bit_length() - 1):
            partner = partner_2(share, "wide", bit_number)
            upper_half = position // 2**bit_number % 2
            share = jnp.where(
                upper_half == 1,
                jnp.concatenate([partner, share], 1),
                jnp.concatenate([share, partner], 1),
            )
        return share

    def project(rows, weight):
        return jnp.dot(rows, weight, preferred_element_type=f32)

    rim = last_of(shifted(normed[-RIM:], "ctx", 1), "wide")
    rim_x = project(rim, w_x).astype(bf16)
    rim_bc = whole_bc(project(rim, w_bc).astype(bf16))
    gates, x_ins, bc_ins, steps = [], [], [], []
    for rows in ring.gather(normed):
        gates.append(project(rows, w_z).astype(bf16))
        x_ins.append(project(rows, w_x).astype(bf16))
        bc_ins.append(whole_bc(project(rows, w_bc).astype(bf16)))
        steps.append(project(rows, w_steps))

    group_index = position // members
    taps_bc = lax.dynamic_slice_in_dim(conv_bc, group_index * 2 * STATE, 2 * STATE, 1)
    fan = jnp.repeat(jnp.eye(heads_here, dtype=bf16), head_dim, axis=1)
    rate = -jnp.exp(a_log)
    shape = jax.ShapeDtypeStruct
    y_local, c_all, cum_all, own_state = call(
        functools.partial(ssd_kernel, sizes),
        [ring.order, *x_ins, *bc_ins, *steps, *(jnp.transpose(s) for s in steps), rim_x, rim_bc]
        + [dt_bias[None], dt_bias[:, None], rate[None], rate[:, None], conv_x, taps_bc]
        + [jnp.repeat(skip, head_dim)[None], fan],
        [
            shape((wide_count, tok_rows, inner_here), f32),
            shape((wide_count, tok_rows, STATE), bf16),
            shape((wide_count, tok_rows, heads_here), f32),
            shape((STATE + 8, inner_here), f32),
        ],
        [
            pltpu.VMEM((wide_count, tok_rows, inner_here), bf16),
            pltpu.VMEM((wide_count, tok_rows, 2 * STATE), bf16),
            pltpu.VMEM((wide_count, tok_rows, heads_here), f32),
            pltpu.VMEM((wide_count, heads_here, tok_rows), f32),
            pltpu.VMEM((RIM, inner_here), f32),
            pltpu.VMEM((RIM, 2 * STATE), f32),
            pltpu.VMEM((STATE, inner_here), f32),
            pltpu.VMEM((1, heads_here), f32),
            pltpu.SemaphoreType.DMA((4, wide_count)),
        ],
        wide_count * 8 * tok_rows * tok_rows * inner_here,
        4 * len(sizes),
    )

    def join(earlier, later):
        return (
            earlier[0] + later[0],
            jnp.exp(later[0]) * earlier[1] + later[1],
        )

    total = (own_state[STATE : STATE + 1], own_state[:STATE])
    prior = (jnp.zeros_like(total[0]), jnp.zeros_like(total[1]))
    for bit_number in range(ctx_count.bit_length() - 1):
        sent = jnp.concatenate([total[1], jnp.broadcast_to(total[0], (8, inner_here))], 0)
        other = partner_2(sent, "ctx", bit_number)
        other = (other[STATE : STATE + 1], other[:STATE])
        upper = ctx_index // 2**bit_number % 2 == 1
        longer = join(other, prior)
        prior = jax.tree.map(lambda a, b: jnp.where(upper, a, b), longer, prior)
        if bit_number + 2 < ctx_count.bit_length():
            total = jax.tree.map(
                lambda a, b: jnp.where(upper, a, b), join(other, total), join(total, other)
            )

    gated = call(
        functools.partial(gate_kernel, sizes),
        [ring.order, y_local, c_all, cum_all, prior[1], norm_gain[None], fan, fan.T, *gates],
        [shape((size * tok_rows, inner_here), bf16) for size in sizes],
        [],
        wide_count * 8 * tok_rows * STATE * inner_here,
    )
    shares = [None] * len(sizes)
    for g in reversed(range(len(sizes))):
        shares[g] = lax.optimization_barrier(project(gated[g], w_out).astype(bf16))
    mamba_out = ring.scatter_sum(shares)
    hidden_stream = (stream + mamba_out).astype(bf16)
    hidden_f32 = hidden_stream.astype(f32)
    moe_in = rms_scale(hidden_f32, moe_gain).astype(bf16)

    def swap(block, distance):
        if distance == 0:
            return block
        route = [(i, i ^ distance) for i in range(ctx_count)]
        return lax.ppermute(block, "ctx", route)

    def cross(rows, size):
        deep = size * capacity
        return jnp.concatenate(
            [swap(rows[d * deep : (d + 1) * deep], d) for d in range(ctx_count)], 0
        )

    results = []
    for g, rows in enumerate(ring.gather(moe_in)):
        picked = project(picks[g], rows).astype(bf16)
        arrived = cross(picked, sizes[g])
        activated = jax.nn.relu(project(arrived, w_up[0]))
        activated = (activated * activated).astype(bf16)
        expert_out = project(activated, w_down[0]).astype(bf16)
        returned = cross(expert_out, sizes[g])
        results.append(
            lax.optimization_barrier(
                lax.dot_general(
                    weighings[g], returned, (((0,), (0,)), ((), ())), preferred_element_type=f32
                ).astype(bf16)
            )
        )
    return (hidden_f32 + ring.scatter_sum(results)).astype(bf16)


def solution(mesh):
    placed = (
        P(("ctx", "wide"), None),
        P(),
        P(None, "wide"),
        P(None, "wide"),
        P(None, "wide"),
        P(),
        P("wide"),
        P("wide"),
        P(None, "wide"),
        P(),
        P("wide"),
        P("wide"),
        P("wide", None),
        P(),
        P(("ctx", "wide"), None),
        P(("ctx", "wide"), None),
        P(("ctx", "wide"), None, None),
        P(("ctx", "wide"), None, None),
    )
    return jax.shard_map(
        shards, mesh=mesh, in_specs=placed, out_specs=P(("ctx", "wide"), None), check_vma=False
    )
```

```python
import jax
import jax.numpy as jnp
from jax import lax
from jax.experimental import pallas as pl
from jax.experimental.pallas import tpu as pltpu
from jax.sharding import PartitionSpec as P

STATE = 128
GROUPS = 8
KERNEL = 4
TOP = 6
RIM = 8

EPSILON = 1e-05
PRECISE = lax.Precision.HIGHEST
LANES = 128
EXPERT_TILE = 512
VMEM_BYTES = 16 * 1024 * 1024


def ring_of(count):
    columns = 1
    while columns * columns * 4 <= count:
        columns *= 2
    rows = count // columns
    if columns == 1 or rows % 2:
        return list(range(count))
    walk = [row * columns for row in range(rows)]
    for lap, row in enumerate(reversed(range(rows))):
        line = list(range(1, columns))
        if lap % 2:
            line.reverse()
        walk += [row * columns + column for column in line]
    return walk


class Ring:
    def __init__(self, count):
        self.count = count
        self.half = count // 2
        self.walk = ring_of(count)
        place = [0] * count
        for spot, index in enumerate(self.walk):
            place[index] = spot
        following = [(self.walk[i], self.walk[(i + 1) % count]) for i in range(count)]
        self.routes = {1: following, -1: [(b, a) for a, b in following]}
        here = jnp.asarray(place, jnp.int32)[lax.axis_index("wide")]
        self.groups = [[0]] + [[s, -s] for s in range(1, self.half)] + [[self.half]]
        self.spots = [sum(len(group) for group in self.groups[:g]) for g in range(self.half + 1)]
        flat = jnp.asarray([o for group in self.groups for o in group], jnp.int32)
        self.order = jnp.asarray(self.walk, jnp.int32)[(here + flat + count) % count]

    def send(self, block, way):
        return lax.ppermute(block, "wide", self.routes[way])

    def forward(self, held, step, halves=True):
        ahead, behind = held[0], held[-1]
        if step + 1 < self.half:
            return [self.send(ahead, -1), self.send(behind, 1)]
        if not halves:
            return [self.send(behind, 1)]
        cut = ahead.shape[0] // 2
        return [self.send(behind[:cut], 1), self.send(ahead[cut:], -1)]

    def pieces(self, rows):
        return [[rows]] + [[rows, rows]] * (self.half - 1) + [[rows // 2, rows - rows // 2]]

    def scatter_sum(self, part):
        far = part(self.half, None)
        up, down = self.send(far[0], 1), self.send(far[1], -1)
        following = part(self.half - 1, far[0])
        for s in range(self.half - 1, 0, -1):
            ahead, behind = add_terms(following, [up, down])
            up, down = self.send(ahead, 1), self.send(behind, -1)
            following = part(s - 1, ahead)
        return [following[0], up, down]


def after(values, *others):
    return lax.optimization_barrier((values, others))[0]


def partner_2(block, axis, bit):
    count = lax.axis_size(axis)
    route = []
    for low in range(count):
        high = low | 1 << bit
        if high != low and high < count:
            route += [(low, high), (high, low)]
    return lax.ppermute(block, axis, route)


def shifted(block, axis, distance):
    devices = range(lax.axis_size(axis))
    route = [(i - distance, i) for i in devices if i - distance in devices]
    return lax.ppermute(block, axis, route)


def doubled(block, axis, bit_number):
    other = partner_2(block, axis, bit_number)
    upper = lax.axis_index(axis) // 2**bit_number % 2 == 1
    return jnp.where(upper, jnp.concatenate([other, block], 0), jnp.concatenate([block, other], 0))


def last_of(block, axis, bit_number):
    other = partner_2(block, axis, bit_number)
    return jnp.where(lax.axis_index(axis) // 2**bit_number % 2 == 1, block, other)


def rms_scale(values, gain_vec):
    mean_sq = jnp.mean(values * values, axis=-1, keepdims=True)
    return values * lax.rsqrt(mean_sq + EPSILON) * gain_vec


def spread(values, fan):
    high = values.astype(jnp.bfloat16)
    low = (values - high.astype(jnp.float32)).astype(jnp.bfloat16)
    return jnp.dot(high, fan, preferred_element_type=jnp.float32) + jnp.dot(
        low, fan, preferred_element_type=jnp.float32
    )


def softplus(values):
    return jnp.maximum(values, 0.0) + jnp.log1p(jnp.exp(-jnp.abs(values)))


def silu(values):
    return values / (1.0 + jnp.exp(-values))


def conv_silu(current, before, taps):
    rows = current.shape[0]
    extended = jnp.concatenate([before, current], 0)
    first = RIM - (KERNEL - 1)
    total = taps[0:1] * extended[first : first + rows]
    for offset in range(1, KERNEL):
        total = total + taps[offset : offset + 1] * extended[first + offset : first + offset + rows]
    return silu(total)


def tile_of(width, limit):
    parts = width // LANES
    return LANES * max(k for k in range(1, parts + 1) if parts % k == 0 and k * LANES <= limit)


def call(kernel, ins, outs, scratch, scalars=0, held=0):
    return pl.pallas_call(
        lambda *refs: kernel(refs),
        out_shape=outs,
        in_specs=[pl.BlockSpec(memory_space=pltpu.SMEM)] * scalars
        + [pl.BlockSpec(memory_space=pltpu.HBM)] * held
        + [pl.BlockSpec(memory_space=pltpu.VMEM)] * (len(ins) - scalars - held),
        out_specs=[pl.BlockSpec(memory_space=pltpu.VMEM)] * len(outs),
        scratch_shapes=scratch,
        compiler_params=pltpu.CompilerParams(vmem_limit_bytes=VMEM_BYTES),
        cost_estimate=BRIEF,
    )(*ins)


BRIEF = pl.CostEstimate(flops=1, bytes_accessed=1, transcendentals=0)
BF16, F32 = jnp.bfloat16, jnp.float32


def dot(a, b):
    return jnp.dot(a, b, preferred_element_type=F32)


def project(pieces, weights, kinds):
    rows = sum(p.shape[0] for p in pieces)
    count, outs = len(pieces), len(weights)

    def kernel(refs):
        parts, weight_refs, out_refs = refs[:count], refs[count : count + outs], refs[count + outs :]
        block = jnp.concatenate([p[...] for p in parts], 0) if count > 1 else parts[0][...]
        for weight, out in zip(weight_refs, out_refs):
            out[...] = dot(block, weight[...]).astype(out.dtype)

    shapes = [jax.ShapeDtypeStruct((rows, w.shape[1]), kind) for w, kind in zip(weights, kinds)]
    return call(kernel, [*pieces, *weights], shapes, [])


def add_terms(own, arrived):
    def kernel(refs):
        ahead, behind, up, down, ahead_out, behind_out = refs
        for term, other, out, last in ((ahead, up, ahead_out, False), (behind, down, behind_out, True)):
            rows, cut = term.shape[0], other.shape[0]
            span = slice(rows - cut, rows) if last else slice(0, cut)
            out[span] = (term[span].astype(F32) + other[...].astype(F32)).astype(out.dtype)
            if cut < rows:
                rest = slice(0, rows - cut) if last else slice(cut, rows)
                out[rest] = term[rest]

    return call(kernel, [*own, *arrived], [jax.ShapeDtypeStruct(p.shape, p.dtype) for p in own], [])


def ssd_span(sizes, rows, heads, order, projected, params):
    pieces = len(sizes)
    count = sum(sizes)
    width = projected[0][0].shape[1]
    head_dim = width // heads
    ins = [order, *(p[0] for p in projected), *(p[1] for p in projected), *(p[2] for p in projected)]
    ins += params

    def kernel(refs):
        order = refs[0]
        x_in, bc_in, steps = (refs[1 + k * pieces : 1 + (k + 1) * pieces] for k in range(3))
        bias, rate, taps_x, taps_bc, skip_row, fan = refs[1 + 3 * pieces : 7 + 3 * pieces]
        refs = refs[7 + 3 * pieces :]
        y_out, c_out, cum_out = (refs[k * pieces : (k + 1) * pieces] for k in range(3))
        starts_out, passed_out, total_out, tails_x, tails_bc, grown, lasts = refs[3 * pieces :]
        row_id = lax.broadcasted_iota(jnp.int32, (rows, rows), 0)
        col_id = lax.broadcasted_iota(jnp.int32, (rows, rows), 1)
        causal = row_id >= col_id
        lower = jnp.where(causal, 1.0, 0.0).astype(F32)
        pair = 2 * head_dim
        left = lax.broadcasted_iota(jnp.int32, (rows, pair), 1) < head_dim
        spots = [(g, j) for g, size in enumerate(sizes) for j in range(size)]
        edge = slice(sizes[-1] * rows, sizes[-1] * rows + 2 * RIM)
        tails_x[0] = x_in[-1][edge].astype(F32)[RIM:]
        tails_bc[0] = bc_in[-1][edge].astype(F32)[RIM:]
        for spot, (g, j) in enumerate(spots):
            edge = slice((j + 1) * rows - 2 * RIM, (j + 1) * rows)
            tails_x[order[spot] + 1] = x_in[g][edge].astype(F32)[RIM:]
            tails_bc[order[spot] + 1] = bc_in[g][edge].astype(F32)[RIM:]
        for spot, (g, j) in enumerate(spots):
            span = slice(j * rows, (j + 1) * rows)
            seq = order[spot]
            x = conv_silu(x_in[g][span].astype(F32), tails_x[seq], taps_x[...])
            bc = conv_silu(bc_in[g][span].astype(F32), tails_bc[seq], taps_bc[...])
            c = bc[:, STATE:].astype(BF16)
            b_t = jnp.transpose(bc[:, :STATE]).astype(BF16)
            dt = softplus(steps[g][span] + bias[...])
            cum = jnp.dot(lower, dt * rate[...], precision=PRECISE, preferred_element_type=F32)
            cum_t = jnp.transpose(cum)
            last = cum[rows - 1 : rows]
            scores = dot(c, b_t)
            x_dt = x * spread(dt, fan[...])
            x_low = x_dt.astype(BF16)
            direct = skip_row[...] * x
            for h in range(0, heads, 2):
                weights = []
                for k in (h, h + 1):
                    gap = cum[:, k : k + 1] - cum_t[k : k + 1, :]
                    weights.append((scores * jnp.exp(jnp.where(causal, gap, -1e30))).astype(BF16))
                units = slice(h * head_dim, h * head_dim + pair)
                both = x_low[:, units]
                none = jnp.zeros_like(both)
                stacked = jnp.concatenate([jnp.where(left, both, none), jnp.where(left, none, both)], 0)
                y_out[g][span, units] = dot(jnp.concatenate(weights, 1), stacked) + direct[:, units]
            tail = (x_dt * spread(jnp.exp(last - cum), fan[...])).astype(BF16)
            grown[seq] = dot(b_t, tail)
            lasts[seq] = jnp.broadcast_to(last, (8, LANES))
            c_out[g][span] = c
            cum_out[g][span] = cum
        state = jnp.zeros((STATE, width), F32)
        passed = jnp.zeros((8, LANES), F32)
        for i in range(count):
            last = lasts[i]
            starts_out[i] = state.astype(BF16)
            passed_out[i] = passed
            state = spread(jnp.exp(last), fan[...])[0:1] * state + grown[i]
            passed = passed + last
        total_out[:STATE] = state
        total_out[STATE:] = spread(passed, fan[...])

    shape = jax.ShapeDtypeStruct
    outs = [shape((size * rows, width), F32) for size in sizes]
    outs += [shape((size * rows, STATE), BF16) for size in sizes]
    outs += [shape((size * rows, LANES), F32) for size in sizes]
    outs += [shape((count, STATE, width), BF16), shape((count, 8, LANES), F32)]
    outs += [shape((STATE + 8, width), F32)]
    scratch = [
        pltpu.VMEM((count + 1, RIM, width), F32),
        pltpu.VMEM((count + 1, RIM, 2 * STATE), F32),
        pltpu.VMEM((count, STATE, width), F32),
        pltpu.VMEM((count, 8, LANES), F32),
    ]
    done = call(kernel, ins, outs, scratch, 1)
    return list(zip(done[:pieces], done[pieces:], done[2 * pieces :])), *done[3 * pieces :]


def route(sizes, rows, deeps, order, peers, choices):
    count = peers.shape[0]

    def kernel(refs):
        order, peers, choices = refs[:3]
        picks, weighings = refs[3 : 3 + len(sizes)], refs[3 + len(sizes) :]
        spot = 0
        for g, size in enumerate(sizes):
            stride = stride_of(deeps[g])
            slots = count * stride
            tokens = size * rows
            parts = []
            for _ in range(size):
                parts.append(choices[pl.ds(pl.multiple_of(order[spot] * rows, rows), rows)])
                spot += 1
            part = jnp.concatenate(parts, 0) if size > 1 else parts[0]
            ids, shares = part[:, :TOP], part[:, TOP : 2 * TOP]
            lane = lax.broadcasted_iota(jnp.int32, (tokens, LANES), 1)
            member = jnp.zeros((tokens, LANES), F32)
            weight = jnp.zeros((tokens, LANES), F32)
            for p in range(count):
                named = ids == peers[p].astype(F32)
                here = jnp.max(jnp.where(named, 1.0, 0.0), axis=1, keepdims=True)
                share = jnp.sum(jnp.where(named, shares, 0.0), axis=1, keepdims=True)
                member = jnp.where(lane == p, here, member)
                weight = jnp.where(lane == p, share, weight)
            row_id = lax.broadcasted_iota(jnp.int32, (tokens, tokens), 0)
            col_id = lax.broadcasted_iota(jnp.int32, (tokens, tokens), 1)
            earlier = jnp.where(row_id > col_id, 1.0, 0.0).astype(BF16)
            rank = jnp.where(member > 0.0, dot(earlier, member.astype(BF16)), -1.0)
            peer_id = lax.broadcasted_iota(jnp.int32, (LANES, slots), 0)
            slot_id = lax.broadcasted_iota(jnp.int32, (LANES, slots), 1)
            first = peer_id * stride
            fan = jnp.where((slot_id >= first) & (slot_id < first + stride), 1.0, 0.0).astype(BF16)
            wanted = lax.rem(lax.broadcasted_iota(jnp.int32, (tokens, slots), 1), stride).astype(F32)
            found = dot(rank.astype(BF16), fan) == wanted
            weighings[g][...] = jnp.where(found, dot(weight.astype(BF16), fan), 0.0).astype(BF16)
            picks[g][...] = jnp.transpose(jnp.where(found, 1.0, 0.0)).astype(BF16)

    shape = jax.ShapeDtypeStruct
    widths = [count * stride_of(deep) for deep in deeps]
    outs = [shape((width, size * rows), BF16) for width, size in zip(widths, sizes)]
    outs += [shape((size * rows, width), BF16) for width, size in zip(widths, sizes)]
    done = call(kernel, [order, peers, choices], outs, [], 2)
    return done[: len(sizes)], done[len(sizes) :]


def gate_and_project(spot, size, piece_rows, head_dim, order, blocks, starts, passed, incoming, params, w_out):
    rows = sum(piece_rows) // size
    ins = [order, *blocks, starts, passed, incoming, *params, w_out]

    def kernel(refs):
        (order, y_ref, c_ref, cum_ref, gate_ref, starts, passed, incoming, gain, fan, fold, w_ref) = refs[:12]
        outs, gated_all = refs[12:-1], refs[-1]
        for j in range(size):
            seq = order[spot + j]
            span = slice(j * rows, (j + 1) * rows)
            fade = spread(jnp.exp(passed[seq]), fan[...])[0:1]
            state = starts[seq].astype(F32) + fade * incoming[...]
            earlier = dot(c_ref[span], state.astype(BF16))
            y = y_ref[span] + spread(jnp.exp(cum_ref[span]), fan[...]) * earlier
            gated = y * silu(gate_ref[span].astype(F32))
            squares = dot((gated * gated).astype(BF16), fold[...])
            scale = lax.rsqrt(squares / head_dim + EPSILON)
            gated_all[span] = (gated * spread(scale, fan[...]) * gain[...]).astype(BF16)
        tile = tile_of(w_ref.shape[1], 1024)
        for n in range(0, w_ref.shape[1], tile):
            columns = slice(n, n + tile)
            share = dot(gated_all[...], w_ref[:, columns]).astype(BF16)
            first = 0
            for out, part in zip(outs, piece_rows):
                out[:, columns] = share[first : first + part]
                first += part

    outs = [jax.ShapeDtypeStruct((part, w_out.shape[1]), BF16) for part in piece_rows]
    return call(kernel, ins, outs, [pltpu.VMEM((size * rows, w_out.shape[0]), BF16)], 1)


def stride_of(deep):
    return -(-deep // 16) * 16


def stack(scratch, pieces):
    deep = pieces[0].shape[0]
    stride = stride_of(deep)
    for k, piece in enumerate(pieces):
        if stride > deep:
            tail = slice(k * stride + deep // 16 * 16, (k + 1) * stride)
            scratch[tail] = jnp.zeros_like(scratch[tail])
        scratch[k * stride : k * stride + deep] = piece[...]


def pick_rows(pieces, picks, deep, peers):
    width = pieces[0].shape[1]
    tile = tile_of(width, 1024)
    count = len(pieces)
    stride = stride_of(deep)

    def kernel(refs):
        parts, pick, outs = refs[:count], refs[count], refs[count + 1 :]
        for n in range(0, width, tile):
            columns = slice(n, n + tile)
            block = [p[:, columns] for p in parts]
            block = jnp.concatenate(block, 0) if count > 1 else block[0]
            rows = dot(pick[...], block).astype(BF16)
            for k, out in enumerate(outs):
                out[:, columns] = rows[k * stride : k * stride + deep]

    return call(kernel, [*pieces, picks], [jax.ShapeDtypeStruct((deep, width), BF16)] * peers, [])


def weigh_rows(returned, weighing, piece_rows):
    deep, width = returned[0].shape
    tile = tile_of(width, 1024)
    count = len(returned)

    def kernel(refs):
        parts, weigh, outs, laid = refs[:count], refs[count], refs[count + 1 : -1], refs[-1]
        stack(laid, parts)
        for n in range(0, width, tile):
            columns = slice(n, n + tile)
            sums = dot(weigh[...], laid[:, columns]).astype(BF16)
            first = 0
            for out, part in zip(outs, piece_rows):
                out[:, columns] = sums[first : first + part]
                first += part

    return call(
        kernel, [*returned, weighing],
        [jax.ShapeDtypeStruct((part, width), BF16) for part in piece_rows],
        [pltpu.VMEM((count * stride_of(deep), width), BF16)],
    )


def held_in_vmem(arrays, parts):
    count = len(arrays)

    def kernel(*refs):
        copies = []
        for k, (source, target) in enumerate(zip(refs[:count], refs[count : 2 * count])):
            rows = source.shape[0] // parts
            for i in range(parts):
                span = pl.ds(i * rows, rows)
                copies.append(
                    pltpu.make_async_copy(source.at[span], target.at[span], refs[-1].at[k, i])
                )
                copies[-1].start()
        for copy in copies:
            copy.wait()

    outs = [jax.ShapeDtypeStruct(a.shape, a.dtype) for a in arrays]
    return call(lambda refs: kernel(*refs), arrays, outs, [pltpu.SemaphoreType.DMA((count, parts))], 0, count)


def run_expert(arrived, w_up_t, w_down):
    deep, width = arrived[0].shape
    hidden = w_down.shape[0]
    tile = tile_of(width, 1024)
    count = len(arrived)
    stride = stride_of(deep)
    rows = count * stride

    def kernel(refs):
        parts, up, down, outs = refs[:count], refs[count], refs[count + 1], refs[count + 2 : -2]
        laid, activated = refs[-2:]
        stack(laid, parts)
        for first in range(0, hidden, EXPERT_TILE):
            units = slice(first, min(first + EXPERT_TILE, hidden))
            positive = jnp.maximum(
                lax.dot_general(
                    laid[...], up[units], (((1,), (1,)), ((), ())), preferred_element_type=F32
                ),
                0.0,
            )
            activated[:, units] = (positive * positive).astype(BF16)
        for n in range(0, width, tile):
            columns = slice(n, n + tile)
            result = dot(activated[...], down[:, columns]).astype(BF16)
            for k, out in enumerate(outs):
                out[:, columns] = result[k * stride : k * stride + deep]

    return call(
        kernel, [*arrived, w_up_t, w_down], [jax.ShapeDtypeStruct((deep, width), BF16)] * count,
        [pltpu.VMEM((rows, width), BF16), pltpu.VMEM((rows, hidden), BF16)],
    )


def shards(
    tokens,
    mamba_gain,
    w_z,
    w_x,
    w_bc,
    w_dt,
    dt_bias,
    a_log,
    conv_x,
    conv_bc,
    skip,
    norm_gain,
    w_out,
    moe_gain,
    expert_ids,
    router_weights,
    w_up,
    w_down,
):
    wide_count = lax.axis_size("wide")
    ctx_count = lax.axis_size("ctx")
    tok_rows, model_width = tokens.shape
    heads_here = dt_bias.shape[0]
    inner_here = w_z.shape[1]
    head_dim = inner_here // heads_here
    position = lax.axis_index("wide")
    ctx_index = lax.axis_index("ctx")
    ring = Ring(wide_count)
    sizes = [len(group) for group in ring.groups]

    stream = tokens.astype(F32)
    normed = rms_scale(stream, mamba_gain).astype(BF16)

    members = wide_count // GROUPS

    def whole_bc(share):
        for bit_number in range(members.bit_length() - 1):
            partner = partner_2(share, "wide", bit_number)
            upper_half = position // 2**bit_number % 2
            share = jnp.where(
                upper_half == 1,
                jnp.concatenate([partner, share], 1),
                jnp.concatenate([share, partner], 1),
            )
        return share

    def per_head(values):
        return jnp.pad(values, (0, LANES - heads_here))[None]

    w_steps = lax.dynamic_slice_in_dim(w_dt, position * heads_here, heads_here, 1)
    w_steps = jnp.pad(w_steps, ((0, 0), (0, LANES - heads_here)))
    group_index = position // members
    taps_bc = lax.dynamic_slice_in_dim(conv_bc, group_index * 2 * STATE, 2 * STATE, 1)
    fan = jnp.repeat(jnp.eye(LANES, heads_here, dtype=BF16), head_dim, axis=1)
    ssd_params = [per_head(dt_bias), per_head(-jnp.exp(a_log)), conv_x, taps_bc]
    ssd_params += [jnp.repeat(skip, head_dim)[None], fan]

    devices = ctx_count * wide_count
    choices = jnp.concatenate([expert_ids.astype(F32), router_weights], 1)
    capacity = max(2, (7 * tok_rows * TOP + 6 * devices - 1) // (6 * devices))
    deeps = [-(-size * capacity // 8) * 8 for size in sizes]
    peers = (ctx_index ^ jnp.arange(ctx_count, dtype=jnp.int32)) * wide_count + position
    bits = wide_count.bit_length() - 1
    hops = [lambda rim: shifted(rim, "ctx", 1)]
    hops += [lambda rim, k=k: last_of(rim, "wide", k) for k in range(bits)]
    hops += [lambda rim: rim] * (ring.half - len(hops))
    gathers = [lambda rows, k=k: doubled(rows, "wide", k) for k in range(bits)]
    gathers += [lambda rows: rows] * (ring.half - len(gathers))

    def mix(held):
        gate, x_in, bc_in, steps = project(held, [w_z, w_x, w_bc, w_steps], [BF16, BF16, BF16, F32])
        return [x_in, whole_bc(bc_in), steps, gate]

    held, rim, projected = [normed], normed[-2 * RIM :], []
    for g in range(ring.half):
        coming = ring.forward(held, g)
        rim, choices = hops[g](rim), gathers[g](choices)
        done = mix(held)
        held, rim, choices, done = lax.optimization_barrier((coming, rim, choices, done))
        projected.append(done)
    for g in range(ring.half, max(len(hops), len(gathers))):
        rim = hops[g](rim) if g < len(hops) else rim
        choices = gathers[g](choices) if g < len(gathers) else choices
    projected.append(mix([*held, rim]))
    blocks, starts, passed, own_state = ssd_span(
        sizes, tok_rows, heads_here, ring.order, projected, ssd_params
    )

    def join(earlier, later):
        return (earlier[0] + later[0], jnp.exp(later[0]) * earlier[1] + later[1])

    total = (own_state[STATE : STATE + 1], own_state[:STATE])
    prior = (jnp.zeros_like(total[0]), jnp.zeros_like(total[1]))
    for bit_number in range(ctx_count.bit_length() - 1):
        sent = own_state
        if bit_number:
            sent = jnp.concatenate([total[1], jnp.broadcast_to(total[0], (8, inner_here))], 0)
        other = partner_2(sent, "ctx", bit_number)
        other = (other[STATE : STATE + 1], other[:STATE])
        upper = ctx_index // 2**bit_number % 2 == 1
        longer = join(other, prior)
        prior = jax.tree.map(lambda a, b: jnp.where(upper, a, b), longer, prior)
        if bit_number + 2 < ctx_count.bit_length():
            total = jax.tree.map(
                lambda a, b: jnp.where(upper, a, b), join(other, total), join(total, other)
            )

    piece_rows = ring.pieces(tok_rows)
    gate_params = [norm_gain[None], fan, fan.T]

    weights = [w_up[0].T, w_down[0]]
    routing = []

    def share(g, token):
        incoming = prior[1] if token is None else after(prior[1], token)
        parts = gate_and_project(
            ring.spots[g], sizes[g], piece_rows[g], head_dim, ring.order, [*blocks[g], projected[g][3]],
            starts, passed, incoming, gate_params, w_out,
        )
        if g == ring.half - 2:
            routing[:] = route(sizes, tok_rows, deeps, ring.order, peers, after(choices, token))
            parts, routing[:] = lax.optimization_barrier((parts, routing))
        if g == max(ring.half - 3, 0):
            weights[:] = held_in_vmem(after(weights, token), 4)
            parts, weights[:] = lax.optimization_barrier((parts, weights))
        return parts

    mamba_out = sum(term.astype(F32) for term in ring.scatter_sum(share))
    picks, weighings = routing
    hidden_stream = (stream + mamba_out).astype(BF16)
    hidden_f32 = hidden_stream.astype(F32)
    moe_in = rms_scale(hidden_f32, moe_gain).astype(BF16)

    def swap(pieces):
        return [
            lax.ppermute(piece, "ctx", [(i, i ^ d) for i in range(ctx_count)]) if d else piece
            for d, piece in enumerate(pieces)
        ]

    held, crossed, expert_outs = [moe_in], None, []
    for g in range(ring.half):
        coming = ring.forward(held, g)
        crossing = swap(pick_rows(held, picks[g], deeps[g], ctx_count))
        done = run_expert(crossed, *weights) if g else None
        held, crossed, done = lax.optimization_barrier((coming, crossing, done))
        expert_outs.append(done)
    crossing = swap(pick_rows(held, picks[-1], deeps[-1], ctx_count))
    done = run_expert(crossed, *weights)
    crossed, done = lax.optimization_barrier((crossing, done))
    expert_outs = expert_outs[1:] + [done, run_expert(crossed, *weights)]

    def result(g, token):
        leaving = expert_outs[g] if token is None else after(expert_outs[g], token)
        return weigh_rows(swap(leaving), weighings[g], piece_rows[g])

    return (hidden_f32 + sum(term.astype(F32) for term in ring.scatter_sum(result))).astype(BF16)


def solution(mesh):
    placed = (
        P(("ctx", "wide"), None),
        P(),
        P(None, "wide"),
        P(None, "wide"),
        P(None, "wide"),
        P(),
        P("wide"),
        P("wide"),
        P(None, "wide"),
        P(),
        P("wide"),
        P("wide"),
        P("wide", None),
        P(),
        P(("ctx", "wide"), None),
        P(("ctx", "wide"), None),
        P(("ctx", "wide"), None, None),
        P(("ctx", "wide"), None, None),
    )
    return jax.shard_map(
        shards, mesh=mesh, in_specs=placed, out_specs=P(("ctx", "wide"), None), check_vma=False
    )
```

```python
import jax
import jax.numpy as jnp
from jax import lax
from jax.experimental import pallas as pl
from jax.experimental.pallas import tpu as pltpu
from jax.sharding import PartitionSpec as P

STATE = 128
GROUPS = 8
KERNEL = 4
TOP = 6
RIM = 8

EPSILON = 1e-05
PRECISE = lax.Precision.HIGHEST
LANES = 128
EXPERT_TILE = 512
VMEM_BYTES = 16 * 1024 * 1024
MOST_VMEM = 56 * 1024 * 1024


def ring_of(count):
    columns = 1
    while columns * columns * 4 <= count:
        columns *= 2
    rows = count // columns
    if columns == 1 or rows % 2:
        return list(range(count))
    walk = [row * columns for row in range(rows)]
    for lap, row in enumerate(reversed(range(rows))):
        line = list(range(1, columns))
        if lap % 2:
            line.reverse()
        walk += [row * columns + column for column in line]
    return walk


class Ring:
    def __init__(self, count):
        self.count = count
        self.half = count // 2
        self.walk = ring_of(count)
        place = [0] * count
        for spot, index in enumerate(self.walk):
            place[index] = spot
        following = [(self.walk[i], self.walk[(i + 1) % count]) for i in range(count)]
        self.routes = {1: following, -1: [(b, a) for a, b in following]}
        here = jnp.asarray(place, jnp.int32)[lax.axis_index("wide")]
        self.groups = [[0]] + [[s, -s] for s in range(1, self.half)] + [[self.half]]
        self.spots = [sum(len(group) for group in self.groups[:g]) for g in range(self.half + 1)]
        flat = jnp.asarray([o for group in self.groups for o in group], jnp.int32)
        self.order = jnp.asarray(self.walk, jnp.int32)[(here + flat + count) % count]

    def send(self, block, way):
        return lax.ppermute(block, "wide", self.routes[way])

    def forward(self, held, step, halves=True):
        ahead, behind = held[0], held[-1]
        if step + 1 < self.half:
            return [self.send(ahead, -1), self.send(behind, 1)]
        if not halves:
            return [self.send(behind, 1)]
        cut = ahead.shape[0] // 2
        return [self.send(behind[:cut], 1), self.send(ahead[cut:], -1)]

    def pieces(self, rows):
        return [[rows]] + [[rows, rows]] * (self.half - 1) + [[rows // 2, rows - rows // 2]]

    def scatter_sum(self, part):
        far = part(self.half, None)
        up, down = self.send(far[0], 1), self.send(far[1], -1)
        following = part(self.half - 1, far[0])
        for s in range(self.half - 1, 0, -1):
            ahead, behind = add_terms(following, [up, down])
            up, down = self.send(ahead, 1), self.send(behind, -1)
            following = part(s - 1, ahead)
        return [following[0], up, down]


def after(values, *others):
    return lax.optimization_barrier((values, others))[0]


def partner_2(block, axis, bit):
    count = lax.axis_size(axis)
    route = []
    for low in range(count):
        high = low | 1 << bit
        if high != low and high < count:
            route += [(low, high), (high, low)]
    return lax.ppermute(block, axis, route)


def shifted(block, axis, distance):
    devices = range(lax.axis_size(axis))
    route = [(i - distance, i) for i in devices if i - distance in devices]
    return lax.ppermute(block, axis, route)


def doubled(block, axis, bit_number):
    other = partner_2(block, axis, bit_number)
    upper = lax.axis_index(axis) // 2**bit_number % 2 == 1
    return jnp.where(upper, jnp.concatenate([other, block], 0), jnp.concatenate([block, other], 0))


def last_of(block, axis, bit_number):
    other = partner_2(block, axis, bit_number)
    return jnp.where(lax.axis_index(axis) // 2**bit_number % 2 == 1, block, other)


def rms_scale(values, gain_vec):
    mean_sq = jnp.mean(values * values, axis=-1, keepdims=True)
    return values * lax.rsqrt(mean_sq + EPSILON) * gain_vec


def spread(values, fan):
    high = values.astype(jnp.bfloat16)
    low = (values - high.astype(jnp.float32)).astype(jnp.bfloat16)
    return jnp.dot(high, fan, preferred_element_type=jnp.float32) + jnp.dot(
        low, fan, preferred_element_type=jnp.float32
    )


def softplus(values):
    return jnp.maximum(values, 0.0) + jnp.log1p(jnp.exp(-jnp.abs(values)))


def silu(values):
    return values / (1.0 + jnp.exp(-values))


def conv_silu(current, before, taps):
    rows = current.shape[0]
    extended = jnp.concatenate([before, current], 0)
    first = RIM - (KERNEL - 1)
    total = taps[0:1] * extended[first : first + rows]
    for offset in range(1, KERNEL):
        total = total + taps[offset : offset + 1] * extended[first + offset : first + offset + rows]
    return silu(total)


def tile_of(width, limit):
    parts = width // LANES
    return LANES * max(k for k in range(1, parts + 1) if parts % k == 0 and k * LANES <= limit)


class Late:
    def __init__(self, source, target, arrival):
        self.target = target
        self.copy = pltpu.make_async_copy(source, target, arrival)
        self.copy.start()
        self.waiting = True

    def __call__(self):
        if self.waiting:
            self.copy.wait()
            self.waiting = False
        return self.target


def call(kernel, ins, outs, scratch, scalars=0, late=0, away=0, room=None):
    def body(*refs):
        refs = list(refs)
        if late:
            arrivals = refs.pop()
            for k in range(late):
                refs[scalars + k] = Late(refs[scalars + k], refs[k - late], arrivals.at[k])
            refs = refs[:-late]
        kernel(refs)

    coming = ins[scalars : scalars + late]
    extra = [pltpu.VMEM(a.shape, a.dtype) for a in coming]
    extra += [pltpu.SemaphoreType.DMA((late,))] if late else []
    return pl.pallas_call(
        body,
        out_shape=outs,
        in_specs=[pl.BlockSpec(memory_space=pltpu.SMEM)] * scalars
        + [pl.BlockSpec(memory_space=pl.ANY)] * late
        + [pl.BlockSpec(memory_space=pltpu.VMEM)] * (len(ins) - scalars - late),
        out_specs=[pl.BlockSpec(memory_space=pl.ANY)] * away
        + [pl.BlockSpec(memory_space=pltpu.VMEM)] * (len(outs) - away),
        scratch_shapes=list(scratch) + extra,
        compiler_params=pltpu.CompilerParams(vmem_limit_bytes=room or VMEM_BYTES),
        cost_estimate=BRIEF,
    )(*ins)


BRIEF = pl.CostEstimate(flops=1, bytes_accessed=1, transcendentals=0)
BF16, F32 = jnp.bfloat16, jnp.float32


def dot(a, b):
    return jnp.dot(a, b, preferred_element_type=F32)


def project(pieces, weights, kinds):
    rows = sum(p.shape[0] for p in pieces)
    count, outs = len(pieces), len(weights)

    def kernel(refs):
        parts, weight_refs, out_refs = refs[:count], refs[count : count + outs], refs[count + outs :]
        block = jnp.concatenate([p[...] for p in parts], 0) if count > 1 else parts[0][...]
        for weight, out in zip(weight_refs, out_refs):
            out[...] = dot(block, weight[...]).astype(out.dtype)

    shapes = [jax.ShapeDtypeStruct((rows, w.shape[1]), kind) for w, kind in zip(weights, kinds)]
    return pl.pallas_call(
        lambda *refs: kernel(refs),
        grid=(1,),
        out_shape=shapes,
        in_specs=[pl.BlockSpec(memory_space=pltpu.VMEM)] * (count + outs),
        out_specs=[pl.BlockSpec(a.shape, lambda i: (0, 0)) for a in shapes],
        compiler_params=pltpu.CompilerParams(vmem_limit_bytes=VMEM_BYTES),
        cost_estimate=BRIEF,
    )(*pieces, *weights)


def add_terms(own, arrived):
    def kernel(refs):
        ahead, behind, up, down, ahead_out, behind_out = refs
        for term, other, out, last in ((ahead, up, ahead_out, False), (behind, down, behind_out, True)):
            rows, cut = term.shape[0], other.shape[0]
            span = slice(rows - cut, rows) if last else slice(0, cut)
            out[span] = (term[span].astype(F32) + other[...].astype(F32)).astype(out.dtype)
            if cut < rows:
                rest = slice(0, rows - cut) if last else slice(cut, rows)
                out[rest] = term[rest]

    return call(kernel, [*own, *arrived], [jax.ShapeDtypeStruct(p.shape, p.dtype) for p in own], [])


def last_rows(sizes, rows, order, projected):
    pieces = len(sizes)
    count = sum(sizes)
    width, more = projected[0][0].shape[1], projected[0][1].shape[1]

    def kernel(refs):
        order, x_in, bc_in = refs[0], refs[1 : 1 + pieces], refs[1 + pieces : 1 + 2 * pieces]
        out, x_edge, bc_edge, arrivals = refs[1 + 2 * pieces :]
        spot = 0
        for g, size in enumerate(sizes):
            for j in range(size):
                edge = pl.ds((j + 1) * rows - 2 * RIM, 2 * RIM)

                @pl.when(order[spot] == count - 1)
                def _(g=g, edge=edge):
                    copies = [
                        pltpu.make_async_copy(x_in[g].at[edge], x_edge, arrivals.at[0]),
                        pltpu.make_async_copy(bc_in[g].at[edge], bc_edge, arrivals.at[1]),
                    ]
                    for copy in copies:
                        copy.start()
                    for copy in copies:
                        copy.wait()

                spot += 1
        out[:, :width] = x_edge[...].astype(F32)[RIM:]
        out[:, width:] = bc_edge[...].astype(F32)[RIM:]

    ins = [order, *(p[0] for p in projected), *(p[1] for p in projected)]
    return pl.pallas_call(
        lambda *refs: kernel(refs),
        out_shape=jax.ShapeDtypeStruct((RIM, width + more), F32),
        in_specs=[pl.BlockSpec(memory_space=pltpu.SMEM)]
        + [pl.BlockSpec(memory_space=pl.ANY)] * (2 * pieces),
        out_specs=pl.BlockSpec(memory_space=pltpu.VMEM),
        scratch_shapes=[
            pltpu.VMEM((2 * RIM, width), BF16),
            pltpu.VMEM((2 * RIM, more), BF16),
            pltpu.SemaphoreType.DMA((2,)),
        ],
        compiler_params=pltpu.CompilerParams(vmem_limit_bytes=MOST_VMEM),
        cost_estimate=BRIEF,
    )(*ins)


def join_states(upper, total, prior, other, last):
    def join(earlier, later):
        state = jnp.exp(later[STATE : STATE + 1]) * earlier[:STATE] + later[:STATE]
        return state, earlier[STATE:] + later[STATE:]

    def kernel(refs):
        upper, total, prior, other, prior_out, total_out = refs

        def put(ref, value):
            ref[:STATE] = value[0].astype(ref.dtype)
            if ref.shape[0] > STATE:
                ref[STATE:] = value[1]

        @pl.when(upper[0] == 1)
        def _():
            put(prior_out, join(other, prior))
            put(total_out, join(other, total))

        @pl.when(upper[0] == 0)
        def _():
            prior_out[...] = prior[...]
            put(total_out, join(total, other))

    shape = jax.ShapeDtypeStruct
    outs = [shape(total.shape, F32)]
    outs += [shape((STATE, total.shape[1]), BF16) if last else shape(total.shape, F32)]
    return call(kernel, [upper, total, prior, other], outs, [], 1)


def ssd_span(sizes, rows, heads, order, projected, rim, params):
    pieces = len(sizes)
    count = sum(sizes)
    width = projected[0][0].shape[1]
    head_dim = width // heads
    ins = [order, *(p[0] for p in projected), *(p[1] for p in projected), *(p[2] for p in projected)]
    ins += [rim, *params]

    def kernel(refs):
        order = refs[0]
        x_in, bc_in, steps = (refs[1 + k * pieces : 1 + (k + 1) * pieces] for k in range(3))
        rim, bias, rate, taps_x, taps_bc, skip_row, fan = refs[1 + 3 * pieces : 8 + 3 * pieces]
        refs = refs[8 + 3 * pieces :]
        y_out, c_out, cum_out = (refs[k * pieces : (k + 1) * pieces] for k in range(3))
        starts_out, passed_out, total_out, tails_x, tails_bc, grown, lasts = refs[3 * pieces : 3 * pieces + 7]
        y_all, c_all, cum_all, starts, passed_all, leaving = refs[3 * pieces + 7 :]
        copies = []

        def take_away(source, target):
            copies.append(pltpu.make_async_copy(source, target, leaving.at[len(copies)]))
            copies[-1].start()

        row_id = lax.broadcasted_iota(jnp.int32, (rows, rows), 0)
        col_id = lax.broadcasted_iota(jnp.int32, (rows, rows), 1)
        causal = row_id >= col_id
        lower = jnp.where(causal, 1.0, 0.0).astype(F32)
        pair = 2 * head_dim
        left = lax.broadcasted_iota(jnp.int32, (rows, pair), 1) < head_dim
        spots = [(g, j) for g, size in enumerate(sizes) for j in range(size)]
        tails_x[0] = rim[:, :width]
        tails_bc[0] = rim[:, width:]
        for spot, (g, j) in enumerate(spots):
            edge = slice((j + 1) * rows - 2 * RIM, (j + 1) * rows)
            tails_x[order[spot] + 1] = x_in[g]()[edge].astype(F32)[RIM:]
            tails_bc[order[spot] + 1] = bc_in[g]()[edge].astype(F32)[RIM:]
        for spot, (g, j) in enumerate(spots):
            span = slice(j * rows, (j + 1) * rows)
            seq = order[spot]
            x = conv_silu(x_in[g]()[span].astype(F32), tails_x[seq], taps_x[...])
            bc = conv_silu(bc_in[g]()[span].astype(F32), tails_bc[seq], taps_bc[...])
            c = bc[:, STATE:].astype(BF16)
            b_t = jnp.transpose(bc[:, :STATE]).astype(BF16)
            dt = softplus(steps[g]()[span] + bias[...])
            cum = jnp.dot(lower, dt * rate[...], precision=PRECISE, preferred_element_type=F32)
            cum_t = jnp.transpose(cum)
            last = cum[rows - 1 : rows]
            scores = dot(c, b_t)
            x_dt = x * spread(dt, fan[...])
            x_low = x_dt.astype(BF16)
            direct = skip_row[...] * x
            for h in range(0, heads, 2):
                weights = []
                for k in (h, h + 1):
                    gap = cum[:, k : k + 1] - cum_t[k : k + 1, :]
                    weights.append((scores * jnp.exp(jnp.where(causal, gap, -1e30))).astype(BF16))
                units = slice(h * head_dim, h * head_dim + pair)
                both = x_low[:, units]
                none = jnp.zeros_like(both)
                stacked = jnp.concatenate([jnp.where(left, both, none), jnp.where(left, none, both)], 0)
                y_all[spot, :, units] = dot(jnp.concatenate(weights, 1), stacked) + direct[:, units]
            tail = (x_dt * spread(jnp.exp(last - cum), fan[...])).astype(BF16)
            grown[seq] = dot(b_t, tail)
            lasts[seq] = jnp.broadcast_to(last, (8, LANES))
            c_all[spot] = c
            cum_all[spot] = cum
            away = pl.ds(j * rows, rows)
            take_away(y_all.at[spot], y_out[g].at[away])
            take_away(c_all.at[spot], c_out[g].at[away])
            take_away(cum_all.at[spot], cum_out[g].at[away])
        state = jnp.zeros((STATE, width), F32)
        passed = jnp.zeros((8, LANES), F32)
        for i in range(count):
            last = lasts[i]
            starts[i] = state.astype(BF16)
            passed_all[i] = passed
            state = spread(jnp.exp(last), fan[...])[0:1] * state + grown[i]
            passed = passed + last
        take_away(starts, starts_out)
        take_away(passed_all, passed_out)
        total_out[:STATE] = state
        total_out[STATE:] = spread(passed, fan[...])
        for copy in copies:
            copy.wait()

    shape = jax.ShapeDtypeStruct
    outs = [shape((size * rows, width), F32) for size in sizes]
    outs += [shape((size * rows, STATE), BF16) for size in sizes]
    outs += [shape((size * rows, LANES), F32) for size in sizes]
    outs += [shape((count, STATE, width), BF16), shape((count, 8, LANES), F32)]
    outs += [shape((STATE + 8, width), F32)]
    scratch = [
        pltpu.VMEM((count + 1, RIM, width), F32),
        pltpu.VMEM((count + 1, RIM, 2 * STATE), F32),
        pltpu.VMEM((count, STATE, width), F32),
        pltpu.VMEM((count, 8, LANES), F32),
        pltpu.VMEM((count, rows, width), F32),
        pltpu.VMEM((count, rows, STATE), BF16),
        pltpu.VMEM((count, rows, LANES), F32),
        pltpu.VMEM((count, STATE, width), BF16),
        pltpu.VMEM((count, 8, LANES), F32),
        pltpu.SemaphoreType.DMA((3 * count + 2,)),
    ]
    done = call(kernel, ins, outs, scratch, 1, 3 * pieces, 3 * pieces + 2, MOST_VMEM)
    return list(zip(done[:pieces], done[pieces:], done[2 * pieces :])), *done[3 * pieces :]


def route(sizes, rows, deeps, order, peers, choices):
    count = peers.shape[0]

    def kernel(refs):
        order, peers, choices = refs[:3]
        picks, weighings = refs[3 : 3 + len(sizes)], refs[3 + len(sizes) :]
        spot = 0
        for g, size in enumerate(sizes):
            stride = stride_of(deeps[g])
            slots = count * stride
            tokens = size * rows
            parts = []
            for _ in range(size):
                parts.append(choices[pl.ds(pl.multiple_of(order[spot] * rows, rows), rows)])
                spot += 1
            part = jnp.concatenate(parts, 0) if size > 1 else parts[0]
            ids, shares = part[:, :TOP], part[:, TOP : 2 * TOP]
            lane = lax.broadcasted_iota(jnp.int32, (tokens, LANES), 1)
            member = jnp.zeros((tokens, LANES), F32)
            weight = jnp.zeros((tokens, LANES), F32)
            for p in range(count):
                named = ids == peers[p].astype(F32)
                here = jnp.max(jnp.where(named, 1.0, 0.0), axis=1, keepdims=True)
                share = jnp.sum(jnp.where(named, shares, 0.0), axis=1, keepdims=True)
                member = jnp.where(lane == p, here, member)
                weight = jnp.where(lane == p, share, weight)
            row_id = lax.broadcasted_iota(jnp.int32, (tokens, tokens), 0)
            col_id = lax.broadcasted_iota(jnp.int32, (tokens, tokens), 1)
            earlier = jnp.where(row_id > col_id, 1.0, 0.0).astype(BF16)
            rank = jnp.where(member > 0.0, dot(earlier, member.astype(BF16)), -1.0)
            peer_id = lax.broadcasted_iota(jnp.int32, (LANES, slots), 0)
            slot_id = lax.broadcasted_iota(jnp.int32, (LANES, slots), 1)
            first = peer_id * stride
            fan = jnp.where((slot_id >= first) & (slot_id < first + stride), 1.0, 0.0).astype(BF16)
            wanted = lax.rem(lax.broadcasted_iota(jnp.int32, (tokens, slots), 1), stride).astype(F32)
            found = dot(rank.astype(BF16), fan) == wanted
            weighings[g][...] = jnp.where(found, dot(weight.astype(BF16), fan), 0.0).astype(BF16)
            picks[g][...] = jnp.transpose(jnp.where(found, 1.0, 0.0)).astype(BF16)

    shape = jax.ShapeDtypeStruct
    widths = [count * stride_of(deep) for deep in deeps]
    outs = [shape((width, size * rows), BF16) for width, size in zip(widths, sizes)]
    outs += [shape((size * rows, width), BF16) for width, size in zip(widths, sizes)]
    done = call(kernel, [order, peers, choices], outs, [], 2)
    return done[: len(sizes)], done[len(sizes) :]


def gate_and_project(spot, size, piece_rows, head_dim, order, upper, blocks, starts, passed, prior, other, params, w_out):
    rows = sum(piece_rows) // size
    ins = [order, upper, *blocks, starts, passed, w_out, prior, other, *params]

    def kernel(refs):
        (order, upper, y_ref, c_ref, cum_ref, gate_ref, starts, passed, w_ref, prior, other, gain, fan, fold) = refs[:14]
        outs, gated_all = refs[14:-1], refs[-1]
        arrived = jnp.exp(prior[STATE : STATE + 1]) * other[...].astype(F32)
        incoming = prior[:STATE] + jnp.where(upper[0] == 1, arrived, 0.0)
        for j in range(size):
            seq = order[spot + j]
            span = slice(j * rows, (j + 1) * rows)
            fade = spread(jnp.exp(passed()[seq]), fan[...])[0:1]
            state = starts()[seq].astype(F32) + fade * incoming
            earlier = dot(c_ref()[span], state.astype(BF16))
            y = y_ref()[span] + spread(jnp.exp(cum_ref()[span]), fan[...]) * earlier
            gated = y * silu(gate_ref()[span].astype(F32))
            squares = dot((gated * gated).astype(BF16), fold[...])
            scale = lax.rsqrt(squares / head_dim + EPSILON)
            gated_all[span] = (gated * spread(scale, fan[...]) * gain[...]).astype(BF16)
        w_ref = w_ref()
        tile = tile_of(w_ref.shape[1], 1024)
        for n in range(0, w_ref.shape[1], tile):
            columns = slice(n, n + tile)
            share = dot(gated_all[...], w_ref[:, columns]).astype(BF16)
            first = 0
            for out, part in zip(outs, piece_rows):
                out[:, columns] = share[first : first + part]
                first += part

    outs = [jax.ShapeDtypeStruct((part, w_out.shape[1]), BF16) for part in piece_rows]
    return call(kernel, ins, outs, [pltpu.VMEM((size * rows, w_out.shape[0]), BF16)], 2, 7, 0, MOST_VMEM)


def stride_of(deep):
    return -(-deep // 16) * 16


def stack(scratch, pieces):
    deep = pieces[0].shape[0]
    stride = stride_of(deep)
    for k, piece in enumerate(pieces):
        if stride > deep:
            tail = slice(k * stride + deep // 16 * 16, (k + 1) * stride)
            scratch[tail] = jnp.zeros_like(scratch[tail])
        scratch[k * stride : k * stride + deep] = piece[...]


def pick_rows(pieces, picks, deep, peers):
    width = pieces[0].shape[1]
    tile = tile_of(width, 1024)
    count = len(pieces)
    stride = stride_of(deep)

    def kernel(refs):
        parts, pick, outs = refs[:count], refs[count], refs[count + 1 :]
        for n in range(0, width, tile):
            columns = slice(n, n + tile)
            block = [p[:, columns] for p in parts]
            block = jnp.concatenate(block, 0) if count > 1 else block[0]
            rows = dot(pick[...], block).astype(BF16)
            for k, out in enumerate(outs):
                out[:, columns] = rows[k * stride : k * stride + deep]

    return call(kernel, [*pieces, picks], [jax.ShapeDtypeStruct((deep, width), BF16)] * peers, [])


def weigh_rows(returned, weighing, piece_rows):
    deep, width = returned[0].shape
    tile = tile_of(width, 1024)
    count = len(returned)

    def kernel(refs):
        parts, weigh, outs, laid = refs[:count], refs[count], refs[count + 1 : -1], refs[-1]
        stack(laid, parts)
        for n in range(0, width, tile):
            columns = slice(n, n + tile)
            sums = dot(weigh[...], laid[:, columns]).astype(BF16)
            first = 0
            for out, part in zip(outs, piece_rows):
                out[:, columns] = sums[first : first + part]
                first += part

    return call(
        kernel, [*returned, weighing],
        [jax.ShapeDtypeStruct((part, width), BF16) for part in piece_rows],
        [pltpu.VMEM((count * stride_of(deep), width), BF16)],
    )


def run_expert(arrived, w_up_t, w_down):
    deep, width = arrived[0].shape
    hidden = w_down.shape[0]
    tile = tile_of(width, 1024)
    count = len(arrived)
    stride = stride_of(deep)
    rows = count * stride

    def kernel(refs):
        parts, up, down, outs = refs[:count], refs[count], refs[count + 1], refs[count + 2 : -2]
        laid, activated = refs[-2:]
        stack(laid, parts)
        for first in range(0, hidden, EXPERT_TILE):
            units = slice(first, min(first + EXPERT_TILE, hidden))
            positive = jnp.maximum(
                lax.dot_general(
                    laid[...], up[units], (((1,), (1,)), ((), ())), preferred_element_type=F32
                ),
                0.0,
            )
            activated[:, units] = (positive * positive).astype(BF16)
        for n in range(0, width, tile):
            columns = slice(n, n + tile)
            result = dot(activated[...], down[:, columns]).astype(BF16)
            for k, out in enumerate(outs):
                out[:, columns] = result[k * stride : k * stride + deep]

    return call(
        kernel, [*arrived, w_up_t, w_down], [jax.ShapeDtypeStruct((deep, width), BF16)] * count,
        [pltpu.VMEM((rows, width), BF16), pltpu.VMEM((rows, hidden), BF16)],
    )


def shards(
    tokens,
    mamba_gain,
    w_z,
    w_x,
    w_bc,
    w_dt,
    dt_bias,
    a_log,
    conv_x,
    conv_bc,
    skip,
    norm_gain,
    w_out,
    moe_gain,
    expert_ids,
    router_weights,
    w_up,
    w_down,
):
    wide_count = lax.axis_size("wide")
    ctx_count = lax.axis_size("ctx")
    tok_rows, model_width = tokens.shape
    heads_here = dt_bias.shape[0]
    inner_here = w_z.shape[1]
    head_dim = inner_here // heads_here
    position = lax.axis_index("wide")
    ctx_index = lax.axis_index("ctx")
    ring = Ring(wide_count)
    sizes = [len(group) for group in ring.groups]

    stream = tokens.astype(F32)
    normed = rms_scale(stream, mamba_gain).astype(BF16)

    members = wide_count // GROUPS

    def whole_bc(share):
        for bit_number in range(members.bit_length() - 1):
            partner = partner_2(share, "wide", bit_number)
            upper_half = position // 2**bit_number % 2
            share = jnp.where(
                upper_half == 1,
                jnp.concatenate([partner, share], 1),
                jnp.concatenate([share, partner], 1),
            )
        return share

    def per_head(values):
        return jnp.pad(values, (0, LANES - heads_here))[None]

    w_steps = lax.dynamic_slice_in_dim(w_dt, position * heads_here, heads_here, 1)
    w_steps = jnp.pad(w_steps, ((0, 0), (0, LANES - heads_here)))
    group_index = position // members
    taps_bc = lax.dynamic_slice_in_dim(conv_bc, group_index * 2 * STATE, 2 * STATE, 1)
    fan = jnp.repeat(jnp.eye(LANES, heads_here, dtype=BF16), head_dim, axis=1)
    ssd_params = [per_head(dt_bias), per_head(-jnp.exp(a_log)), conv_x, taps_bc]
    ssd_params += [jnp.repeat(skip, head_dim)[None], fan]

    devices = ctx_count * wide_count
    choices = jnp.concatenate([expert_ids.astype(F32), router_weights], 1)
    capacity = max(2, (7 * tok_rows * TOP + 6 * devices - 1) // (6 * devices))
    deeps = [-(-size * capacity // 8) * 8 for size in sizes]
    peers = (ctx_index ^ jnp.arange(ctx_count, dtype=jnp.int32)) * wide_count + position
    bits = wide_count.bit_length() - 1
    def mix(held):
        gate, x_in, bc_in, steps = project(held, [w_z, w_x, w_bc, w_steps], [BF16, BF16, BF16, F32])
        return [x_in, whole_bc(bc_in), steps, gate]

    held, projected = [normed], []
    for g in range(ring.half):
        coming = ring.forward(held, g)
        done = mix(held)
        held, done = lax.optimization_barrier((coming, done))
        projected.append(done)
    projected.append(mix(held))
    rim = last_rows(sizes, tok_rows, ring.order, projected)
    choices = after(choices, rim)
    rim, choices = lax.optimization_barrier((shifted(rim, "ctx", 1), doubled(choices, "wide", 0)))
    blocks, starts, passed, total = ssd_span(
        sizes, tok_rows, heads_here, ring.order, projected, rim, ssd_params
    )

    prior = jnp.zeros_like(total)
    scans = ctx_count.bit_length() - 1

    def beside(crossing, choices, lap):
        if lap < bits:
            choices = doubled(choices, "wide", lap)
        return lax.optimization_barrier((crossing, choices))

    for bit_number in range(scans - 1):
        upper = (ctx_index // 2**bit_number % 2)[None]
        total, choices = lax.optimization_barrier((total, choices))
        other, choices = beside(partner_2(total, "ctx", bit_number), choices, 1 + bit_number)
        prior, total = join_states(upper, total, prior, other, bit_number == scans - 2)
    upper = (ctx_index // 2 ** (scans - 1) % 2)[None]
    total, choices = lax.optimization_barrier((total, choices))
    other, choices = beside(partner_2(total[:STATE], "ctx", scans - 1), choices, scans)
    for lap in range(1 + scans, bits):
        choices = doubled(choices, "wide", lap)

    piece_rows = ring.pieces(tok_rows)
    gate_params = [norm_gain[None], fan, fan.T]

    weights = [w_up[0].T, w_down[0]]
    routing = []

    def share(g, token):
        entering = prior if token is None else after(prior, token)
        parts = gate_and_project(
            ring.spots[g], sizes[g], piece_rows[g], head_dim, ring.order, upper, [*blocks[g], projected[g][3]],
            starts, passed, entering, other, gate_params, w_out,
        )
        if g == max(ring.half - 2, 0):
            routing[:] = route(sizes, tok_rows, deeps, ring.order, peers, after(choices, token))
            parts, routing[:] = lax.optimization_barrier((parts, routing))
        return parts

    terms = ring.scatter_sum(share)
    picks, weighings = routing
    mamba_out = sum(term.astype(F32) for term in terms)
    hidden_stream = (stream + mamba_out).astype(BF16)
    hidden_f32 = hidden_stream.astype(F32)
    moe_in = rms_scale(hidden_f32, moe_gain).astype(BF16)

    def swap(pieces):
        return [
            lax.ppermute(piece, "ctx", [(i, i ^ d) for i in range(ctx_count)]) if d else piece
            for d, piece in enumerate(pieces)
        ]

    held, crossed, expert_outs = [moe_in], None, []
    for g in range(ring.half):
        coming = ring.forward(held, g)
        crossing = swap(pick_rows(held, picks[g], deeps[g], ctx_count))
        done = run_expert(crossed, *weights) if g else None
        held, crossed, done = lax.optimization_barrier((coming, crossing, done))
        expert_outs.append(done)
    crossing = swap(pick_rows(held, picks[-1], deeps[-1], ctx_count))
    done = run_expert(crossed, *weights)
    crossed, done = lax.optimization_barrier((crossing, done))
    expert_outs = expert_outs[1:] + [done, run_expert(crossed, *weights)]

    def result(g, token):
        leaving = expert_outs[g] if token is None else after(expert_outs[g], token)
        return weigh_rows(swap(leaving), weighings[g], piece_rows[g])

    return (hidden_f32 + sum(term.astype(F32) for term in ring.scatter_sum(result))).astype(BF16)


def solution(mesh):
    placed = (
        P(("ctx", "wide"), None),
        P(),
        P(None, "wide"),
        P(None, "wide"),
        P(None, "wide"),
        P(),
        P("wide"),
        P("wide"),
        P(None, "wide"),
        P(),
        P("wide"),
        P("wide"),
        P("wide", None),
        P(),
        P(("ctx", "wide"), None),
        P(("ctx", "wide"), None),
        P(("ctx", "wide"), None, None),
        P(("ctx", "wide"), None, None),
    )
    return jax.shard_map(
        shards, mesh=mesh, in_specs=placed, out_specs=P(("ctx", "wide"), None), check_vma=False
    )
```

```python
import jax
import jax.numpy as jnp
from jax import lax
from jax.experimental import pallas as pl
from jax.experimental.pallas import tpu as pltpu
from jax.sharding import PartitionSpec as P

STATE = 128
GROUPS = 8
KERNEL = 4
TOP = 6
RIM = 8

EPSILON = 1e-05
PRECISE = lax.Precision.HIGHEST
LANES = 128
EXPERT_TILE = 512
VMEM_BYTES = 16 * 1024 * 1024
MOST_VMEM = 56 * 1024 * 1024


def ring_of(count):
    columns = 1
    while columns * columns * 4 <= count:
        columns *= 2
    rows = count // columns
    if columns == 1 or rows % 2:
        return list(range(count))
    walk = [row * columns for row in range(rows)]
    for lap, row in enumerate(reversed(range(rows))):
        line = list(range(1, columns))
        if lap % 2:
            line.reverse()
        walk += [row * columns + column for column in line]
    return walk


class Ring:
    def __init__(self, count):
        self.count = count
        self.half = count // 2
        self.walk = ring_of(count)
        place = [0] * count
        for spot, index in enumerate(self.walk):
            place[index] = spot
        following = [(self.walk[i], self.walk[(i + 1) % count]) for i in range(count)]
        self.routes = {1: following, -1: [(b, a) for a, b in following]}
        here = jnp.asarray(place, jnp.int32)[lax.axis_index("wide")]
        self.groups = [[0]] + [[s, -s] for s in range(1, self.half)] + [[self.half]]
        self.spots = [sum(len(group) for group in self.groups[:g]) for g in range(self.half + 1)]
        flat = jnp.asarray([o for group in self.groups for o in group], jnp.int32)
        self.order = jnp.asarray(self.walk, jnp.int32)[(here + flat + count) % count]

    def send(self, block, way):
        return lax.ppermute(block, "wide", self.routes[way])

    def forward(self, held, step, halves=True):
        ahead, behind = held[0], held[-1]
        if step + 1 < self.half:
            return [self.send(ahead, -1), self.send(behind, 1)]
        if not halves:
            return [self.send(behind, 1)]
        cut = ahead.shape[0] // 2
        return [self.send(behind[:cut], 1), self.send(ahead[cut:], -1)]

    def pieces(self, rows):
        return [[rows]] + [[rows, rows]] * (self.half - 1) + [[rows // 2, rows - rows // 2]]

    def scatter_sum(self, part, late):
        far = part(self.half, None)
        up, down = self.send(far[0], 1), self.send(far[1], -1)
        following = part(self.half - 1, far[0])
        for s in range(self.half - 1, 0, -1):
            ahead, behind = add_terms(following, [up, down], late)
            up, down = self.send(ahead, 1), self.send(behind, -1)
            following = part(s - 1, ahead)
        return [following[0], up, down]


def after(values, *others):
    return lax.optimization_barrier((values, others))[0]


def partner_2(block, axis, bit):
    count = lax.axis_size(axis)
    route = []
    for low in range(count):
        high = low | 1 << bit
        if high != low and high < count:
            route += [(low, high), (high, low)]
    return lax.ppermute(block, axis, route)


def shifted(block, axis, distance):
    devices = range(lax.axis_size(axis))
    route = [(i - distance, i) for i in devices if i - distance in devices]
    return lax.ppermute(block, axis, route)


def fan_of(heads, head_dim):
    head_id = lax.broadcasted_iota(jnp.int32, (LANES, heads * head_dim), 0)
    first = head_id * head_dim
    unit_id = lax.broadcasted_iota(jnp.int32, (LANES, heads * head_dim), 1)
    return jnp.where((unit_id >= first) & (unit_id < first + head_dim), 1.0, 0.0).astype(BF16)


def spread(values, fan):
    high = values.astype(jnp.bfloat16)
    low = (values - high.astype(jnp.float32)).astype(jnp.bfloat16)
    return jnp.dot(high, fan, preferred_element_type=jnp.float32) + jnp.dot(
        low, fan, preferred_element_type=jnp.float32
    )


def softplus(values):
    return jnp.maximum(values, 0.0) + jnp.log1p(jnp.exp(-jnp.abs(values)))


def silu(values):
    return values / (1.0 + jnp.exp(-values))


def conv_silu(current, before, taps):
    rows = current.shape[0]
    extended = jnp.concatenate([before, current], 0)
    first = RIM - (KERNEL - 1)
    total = taps[0:1] * extended[first : first + rows]
    for offset in range(1, KERNEL):
        total = total + taps[offset : offset + 1] * extended[first + offset : first + offset + rows]
    return silu(total)


def tile_of(width, limit):
    parts = width // LANES
    return LANES * max(k for k in range(1, parts + 1) if parts % k == 0 and k * LANES <= limit)


class Late:
    def __init__(self, source, target, arrival):
        self.target = target
        self.copy = pltpu.make_async_copy(source, target, arrival)
        self.copy.start()
        self.waiting = True

    def __call__(self):
        if self.waiting:
            self.copy.wait()
            self.waiting = False
        return self.target


def call(kernel, ins, outs, scratch, scalars=0, late=0, away=0, room=None):
    def body(*refs):
        refs = list(refs)
        if late:
            arrivals = refs.pop()
            for k in range(late):
                refs[scalars + k] = Late(refs[scalars + k], refs[k - late], arrivals.at[k])
            refs = refs[:-late]
        kernel(refs)

    coming = ins[scalars : scalars + late]
    extra = [pltpu.VMEM(a.shape, a.dtype) for a in coming]
    extra += [pltpu.SemaphoreType.DMA((late,))] if late else []
    return pl.pallas_call(
        body,
        out_shape=outs,
        in_specs=[pl.BlockSpec(memory_space=pltpu.SMEM)] * scalars
        + [pl.BlockSpec(memory_space=pl.ANY)] * late
        + [pl.BlockSpec(memory_space=pltpu.VMEM)] * (len(ins) - scalars - late),
        out_specs=[pl.BlockSpec(memory_space=pl.ANY)] * away
        + [pl.BlockSpec(memory_space=pltpu.VMEM)] * (len(outs) - away),
        scratch_shapes=list(scratch) + extra,
        compiler_params=pltpu.CompilerParams(vmem_limit_bytes=room or VMEM_BYTES),
        cost_estimate=BRIEF,
    )(*ins)


BRIEF = pl.CostEstimate(flops=1, bytes_accessed=1, transcendentals=0)
BF16, F32 = jnp.bfloat16, jnp.float32


def dot(a, b):
    return jnp.dot(a, b, preferred_element_type=F32)


def normed_with_marks(tokens, gain, marks):
    rows, width = tokens.shape

    def kernel(refs):
        tokens, gain, marks, out = refs
        values = tokens[...].astype(F32)
        mean_sq = jnp.sum(values * values, axis=1, keepdims=True) / width
        out[:, :width] = (values * lax.rsqrt(mean_sq + EPSILON) * gain[...]).astype(BF16)
        out[:, width:] = marks[...]

    outs = [jax.ShapeDtypeStruct((rows, width + LANES), BF16)]
    return call(kernel, [tokens, gain[None], marks], outs, [])[0]


def project(pieces, weights, order=None, sizes=(), earlier=()):
    rows = sum(p.shape[0] for p in pieces)
    depth = weights[0].shape[0]
    count, outs = len(pieces), len(weights)
    count_all = sum(sizes)
    block_rows = rows // sizes[-1] if sizes else 0
    scalars = [order] if sizes else []
    far = [p[k] for k in (1, 2) for p in earlier]
    ins = [*scalars, *far, *pieces, *weights]

    def kernel(*refs):
        order, refs = (refs[0], refs[1:]) if sizes else (None, refs)
        edges, refs = refs[: len(far)], refs[len(far) :]
        parts, weight_refs = refs[:count], refs[count : count + outs]
        out_refs = refs[count + outs : count + 2 * outs + 1]
        if sizes:
            rim, x_edge, bc_edge, arrivals = refs[count + 2 * outs + 1 :]
            spot = 0
            for g, size in enumerate(sizes[:-1]):
                for j in range(size):
                    edge = pl.ds((j + 1) * block_rows - 2 * RIM, 2 * RIM)

                    @pl.when(order[spot] == count_all - 1)
                    def _(g=g, edge=edge):
                        copies = [
                            pltpu.make_async_copy(edges[g].at[edge], x_edge, arrivals.at[0]),
                            pltpu.make_async_copy(edges[len(earlier) + g].at[edge], bc_edge, arrivals.at[1]),
                        ]
                        for copy in copies:
                            copy.start()
                        for copy in copies:
                            copy.wait()

                    spot += 1
        block = [p[:, :depth] for p in parts]
        block = jnp.concatenate(block, 0) if count > 1 else block[0]
        for weight, out in zip(weight_refs, out_refs):
            out[...] = dot(block, weight[...]).astype(out.dtype)
        first = 0
        for p in parts:
            out_refs[-1][first : first + p.shape[0]] = p[:, depth:]
            first += p.shape[0]
        if sizes:

            @pl.when(order[spot] == count_all - 1)
            def _():
                x_edge[...] = out_refs[1][rows - 2 * RIM :]
                bc_edge[...] = out_refs[2][rows - 2 * RIM :]

            rim[:, : x_edge.shape[1]] = x_edge[...].astype(F32)[RIM:]
            rim[:, x_edge.shape[1] :] = bc_edge[...].astype(F32)[RIM:]

    shape = jax.ShapeDtypeStruct
    widths = [w.shape[1] for w in weights]
    shapes = [shape((rows, width), BF16) for width in widths[:-1]]
    shapes += [shape((rows, widths[-1]), F32), shape((rows, LANES), BF16)]
    scratch = []
    if sizes:
        shapes.append(shape((RIM, widths[1] + widths[2]), F32))
        scratch = [
            pltpu.VMEM((2 * RIM, widths[1]), BF16),
            pltpu.VMEM((2 * RIM, widths[2]), BF16),
            pltpu.SemaphoreType.DMA((2,)),
        ]
    return pl.pallas_call(
        kernel,
        grid=(1,),
        out_shape=shapes,
        in_specs=[pl.BlockSpec(memory_space=pltpu.SMEM)] * len(scalars)
        + [pl.BlockSpec(memory_space=pl.ANY)] * len(far)
        + [pl.BlockSpec(memory_space=pltpu.VMEM)] * (count + outs),
        out_specs=[pl.BlockSpec(a.shape, lambda i: (0, 0)) for a in shapes],
        scratch_shapes=scratch,
        compiler_params=pltpu.CompilerParams(vmem_limit_bytes=VMEM_BYTES),
        cost_estimate=BRIEF,
    )(*ins)


def add_terms(own, arrived, late):
    def kernel(refs):
        ahead, behind, up, down, ahead_out, behind_out = refs
        for term, other, out, last in ((ahead, up, ahead_out, False), (behind, down, behind_out, True)):
            term = term() if late else term
            rows, cut = term.shape[0], other.shape[0]
            span = slice(rows - cut, rows) if last else slice(0, cut)
            out[span] = (term[span].astype(F32) + other[...].astype(F32)).astype(out.dtype)
            if cut < rows:
                rest = slice(0, rows - cut) if last else slice(cut, rows)
                out[rest] = term[rest]

    outs = [jax.ShapeDtypeStruct(p.shape, p.dtype) for p in own]
    if late:
        return call(kernel, [*own, *arrived], outs, [], 0, 2, 0, MOST_VMEM)
    return call(kernel, [*own, *arrived], outs, [])


def hidden_and_normed(tokens, terms, gain):
    def kernel(refs):
        tokens, own, up, down, gain, hidden_out, normed_out = refs
        total = own[...].astype(F32) + up[...].astype(F32) + down[...].astype(F32)
        hidden = (tokens[...].astype(F32) + total).astype(BF16)
        hidden_out[...] = hidden
        hidden = hidden.astype(F32)
        mean_sq = jnp.sum(hidden * hidden, axis=1, keepdims=True) / tokens.shape[1]
        normed_out[...] = (hidden * lax.rsqrt(mean_sq + EPSILON) * gain[...]).astype(BF16)

    outs = [jax.ShapeDtypeStruct(tokens.shape, BF16)] * 2
    return call(kernel, [tokens, *terms, gain[None]], outs, [])


def last_rows(sizes, rows, order, projected):
    found = 0.0
    spot = 0
    for g, size in enumerate(sizes):
        for j in range(size):
            edge = slice((j + 1) * rows - RIM, (j + 1) * rows)
            both = jnp.concatenate([projected[g][1][edge], projected[g][2][edge]], 1).astype(F32)
            found = found + jnp.where(order[spot] == sum(sizes) - 1, both, 0.0)
            spot += 1
    return found


def join_states(upper, total, prior, other, last):
    def join(earlier, later):
        state = jnp.exp(later[STATE : STATE + 1]) * earlier[:STATE] + later[:STATE]
        return state, earlier[STATE:] + later[STATE:]

    def kernel(refs):
        upper, total, prior, other, prior_out, total_out = refs

        def put(ref, value):
            ref[:STATE] = value[0].astype(ref.dtype)
            if ref.shape[0] > STATE:
                ref[STATE:] = value[1]

        @pl.when(upper[0] == 1)
        def _():
            put(prior_out, join(other, prior))
            put(total_out, join(other, total))

        @pl.when(upper[0] == 0)
        def _():
            prior_out[...] = prior[...]
            put(total_out, join(total, other))

    shape = jax.ShapeDtypeStruct
    outs = [shape(total.shape, F32)]
    outs += [shape((STATE, total.shape[1]), BF16) if last else shape(total.shape, F32)]
    return call(kernel, [upper, total, prior, other], outs, [], 1)


def ssd_span(sizes, rows, heads, order, projected, rim, params):
    pieces = len(sizes)
    count = sum(sizes)
    width = projected[0][1].shape[1]
    head_dim = width // heads
    ins = [order, *(p[k] for k in (1, 2, 3) for p in projected[:-1])]
    ins += [projected[-1][k] for k in (1, 2, 3)] + [rim, *params]

    def kernel(refs):
        order = refs[0]
        before = pieces - 1
        x_in, bc_in, steps = (
            [*refs[1 + k * before : 1 + (k + 1) * before], refs[1 + 3 * before + k]] for k in range(3)
        )
        rim, bias, rate, taps_x, taps_bc, skip_heads = refs[1 + 3 * pieces : 7 + 3 * pieces]
        refs = refs[7 + 3 * pieces :]
        fan = fan_of(heads, head_dim)
        skip_row = spread(jnp.broadcast_to(skip_heads[...], (8, LANES)), fan)[0:1]
        x_in, bc_in, steps = ([*arrays[:-1], lambda last=arrays[-1]: last] for arrays in (x_in, bc_in, steps))
        y_out, c_out, cum_out = (refs[k * pieces : (k + 1) * pieces] for k in range(3))
        starts_out, passed_out, total_out, tails_x, tails_bc, grown, lasts = refs[3 * pieces : 3 * pieces + 7]
        y_all, c_all, cum_all, starts, passed_all, leaving = refs[3 * pieces + 7 :]
        copies = []

        def take_away(source, target):
            copies.append(pltpu.make_async_copy(source, target, leaving.at[len(copies)]))
            copies[-1].start()

        row_id = lax.broadcasted_iota(jnp.int32, (rows, rows), 0)
        col_id = lax.broadcasted_iota(jnp.int32, (rows, rows), 1)
        causal = row_id >= col_id
        lower = jnp.where(causal, 1.0, 0.0).astype(F32)
        pair = 2 * head_dim
        left = lax.broadcasted_iota(jnp.int32, (rows, pair), 1) < head_dim
        spots = [(g, j) for g, size in enumerate(sizes) for j in range(size)]
        tails_x[0] = rim[:, :width]
        tails_bc[0] = rim[:, width:]
        for spot, (g, j) in enumerate(spots):
            edge = slice((j + 1) * rows - 2 * RIM, (j + 1) * rows)
            tails_x[order[spot] + 1] = x_in[g]()[edge].astype(F32)[RIM:]
            tails_bc[order[spot] + 1] = bc_in[g]()[edge].astype(F32)[RIM:]
        for spot, (g, j) in enumerate(spots):
            span = slice(j * rows, (j + 1) * rows)
            seq = order[spot]
            x = conv_silu(x_in[g]()[span].astype(F32), tails_x[seq], taps_x[...])
            bc = conv_silu(bc_in[g]()[span].astype(F32), tails_bc[seq], taps_bc[...])
            c = bc[:, STATE:].astype(BF16)
            b_t = jnp.transpose(bc[:, :STATE]).astype(BF16)
            dt = softplus(steps[g]()[span] + bias[...])
            cum = jnp.dot(lower, dt * rate[...], precision=PRECISE, preferred_element_type=F32)
            cum_t = jnp.transpose(cum)
            last = cum[rows - 1 : rows]
            scores = dot(c, b_t)
            x_dt = x * spread(dt, fan)
            x_low = x_dt.astype(BF16)
            direct = skip_row * x
            for h in range(0, heads, 2):
                weights = []
                for k in (h, h + 1):
                    gap = cum[:, k : k + 1] - cum_t[k : k + 1, :]
                    weights.append((scores * jnp.exp(jnp.where(causal, gap, -1e30))).astype(BF16))
                units = slice(h * head_dim, h * head_dim + pair)
                both = x_low[:, units]
                none = jnp.zeros_like(both)
                stacked = jnp.concatenate([jnp.where(left, both, none), jnp.where(left, none, both)], 0)
                y_all[spot, :, units] = dot(jnp.concatenate(weights, 1), stacked) + direct[:, units]
            tail = (x_dt * spread(jnp.exp(last - cum), fan)).astype(BF16)
            grown[seq] = dot(b_t, tail)
            lasts[seq] = jnp.broadcast_to(last, (8, LANES))
            c_all[spot] = c
            cum_all[spot] = cum
            away = pl.ds(j * rows, rows)
            take_away(y_all.at[spot], y_out[g].at[away])
            take_away(c_all.at[spot], c_out[g].at[away])
            take_away(cum_all.at[spot], cum_out[g].at[away])
        state = jnp.zeros((STATE, width), F32)
        passed = jnp.zeros((8, LANES), F32)
        for i in range(count):
            last = lasts[i]
            starts[i] = state.astype(BF16)
            passed_all[i] = passed
            state = spread(jnp.exp(last), fan)[0:1] * state + grown[i]
            passed = passed + last
        take_away(starts, starts_out)
        take_away(passed_all, passed_out)
        total_out[:STATE] = state
        total_out[STATE:] = spread(passed, fan)
        for copy in copies:
            copy.wait()

    shape = jax.ShapeDtypeStruct
    outs = [shape((size * rows, width), F32) for size in sizes]
    outs += [shape((size * rows, STATE), BF16) for size in sizes]
    outs += [shape((size * rows, LANES), F32) for size in sizes]
    outs += [shape((count, STATE, width), BF16), shape((count, 8, LANES), F32)]
    outs += [shape((STATE + 8, width), F32)]
    scratch = [
        pltpu.VMEM((count + 1, RIM, width), F32),
        pltpu.VMEM((count + 1, RIM, 2 * STATE), F32),
        pltpu.VMEM((count, STATE, width), F32),
        pltpu.VMEM((count, 8, LANES), F32),
        pltpu.VMEM((count, rows, width), F32),
        pltpu.VMEM((count, rows, STATE), BF16),
        pltpu.VMEM((count, rows, LANES), F32),
        pltpu.VMEM((count, STATE, width), BF16),
        pltpu.VMEM((count, 8, LANES), F32),
        pltpu.SemaphoreType.DMA((3 * count + 2,)),
    ]
    done = call(kernel, ins, outs, scratch, 1, 3 * (pieces - 1), 3 * pieces + 2, MOST_VMEM)
    return list(zip(done[:pieces], done[pieces:], done[2 * pieces :])), *done[3 * pieces :]


def route(sizes, rows, deeps, peers, marks):
    count = peers.shape[0]

    def kernel(refs):
        peers, marks = refs[0], refs[1 : 1 + len(sizes)]
        picks, weighings = refs[1 + len(sizes) : 1 + 2 * len(sizes)], refs[1 + 2 * len(sizes) :]
        for g, size in enumerate(sizes):
            stride = stride_of(deeps[g])
            slots = count * stride
            tokens = size * rows
            part = marks[g][...].astype(F32)
            columns = [part[:, k * TOP : (k + 1) * TOP] for k in range(4)]
            ids, shares = columns[0] * LANES + columns[1], columns[2] + columns[3]
            lane = lax.broadcasted_iota(jnp.int32, (tokens, LANES), 1)
            member = jnp.zeros((tokens, LANES), F32)
            weight = jnp.zeros((tokens, LANES), F32)
            for p in range(count):
                named = ids == peers[p].astype(F32)
                here = jnp.max(jnp.where(named, 1.0, 0.0), axis=1, keepdims=True)
                share = jnp.sum(jnp.where(named, shares, 0.0), axis=1, keepdims=True)
                member = jnp.where(lane == p, here, member)
                weight = jnp.where(lane == p, share, weight)
            row_id = lax.broadcasted_iota(jnp.int32, (tokens, tokens), 0)
            col_id = lax.broadcasted_iota(jnp.int32, (tokens, tokens), 1)
            earlier = jnp.where(row_id > col_id, 1.0, 0.0).astype(BF16)
            rank = jnp.where(member > 0.0, dot(earlier, member.astype(BF16)), -1.0)
            peer_id = lax.broadcasted_iota(jnp.int32, (LANES, slots), 0)
            slot_id = lax.broadcasted_iota(jnp.int32, (LANES, slots), 1)
            first = peer_id * stride
            fan = jnp.where((slot_id >= first) & (slot_id < first + stride), 1.0, 0.0).astype(BF16)
            wanted = lax.rem(lax.broadcasted_iota(jnp.int32, (tokens, slots), 1), stride).astype(F32)
            found = dot(rank.astype(BF16), fan) == wanted
            weighings[g][...] = jnp.where(found, dot(weight.astype(BF16), fan), 0.0).astype(BF16)
            picks[g][...] = jnp.transpose(jnp.where(found, 1.0, 0.0)).astype(BF16)

    shape = jax.ShapeDtypeStruct
    widths = [count * stride_of(deep) for deep in deeps]
    outs = [shape((width, size * rows), BF16) for width, size in zip(widths, sizes)]
    outs += [shape((size * rows, width), BF16) for width, size in zip(widths, sizes)]
    done = call(kernel, [peers, *marks], outs, [], 1)
    return done[: len(sizes)], done[len(sizes) :]


def gate_and_project(spot, size, piece_rows, head_dim, order, upper, blocks, starts, passed, prior, other, params, w_out, room):
    rows = sum(piece_rows) // size
    ins = [order, upper, *blocks, starts, passed, w_out, prior, other, *params]

    def kernel(refs):
        (order, upper, y_ref, c_ref, cum_ref, gate_ref, starts, passed, w_ref, prior, other, gain) = refs[:12]
        outs, gated_all = refs[12:-1], refs[-1]
        fan = fan_of(w_out.shape[0] // head_dim, head_dim)
        arrived = jnp.exp(prior[STATE : STATE + 1]) * other[...].astype(F32)
        incoming = prior[:STATE] + jnp.where(upper[0] == 1, arrived, 0.0)
        for j in range(size):
            seq = order[spot + j]
            span = slice(j * rows, (j + 1) * rows)
            fade = spread(jnp.exp(passed()[seq]), fan)[0:1]
            state = starts()[seq].astype(F32) + fade * incoming
            earlier = dot(c_ref()[span], state.astype(BF16))
            y = y_ref()[span] + spread(jnp.exp(cum_ref()[span]), fan) * earlier
            gated = y * silu(gate_ref()[span].astype(F32))
            squares = lax.dot_general(
                (gated * gated).astype(BF16), fan, (((1,), (1,)), ((), ())), preferred_element_type=F32
            )
            scale = lax.rsqrt(squares / head_dim + EPSILON)
            gated_all[span] = (gated * spread(scale, fan) * gain[...]).astype(BF16)
        w_ref = w_ref()
        tile = tile_of(w_ref.shape[1], 1024)
        for n in range(0, w_ref.shape[1], tile):
            columns = slice(n, n + tile)
            share = dot(gated_all[...], w_ref[:, columns]).astype(BF16)
            first = 0
            for out, part in zip(outs, piece_rows):
                out[:, columns] = share[first : first + part]
                first += part

    outs = [jax.ShapeDtypeStruct((part, w_out.shape[1]), BF16) for part in piece_rows]
    return call(kernel, ins, outs, [pltpu.VMEM((size * rows, w_out.shape[0]), BF16)], 2, 7, 0, room)


def stride_of(deep):
    return -(-deep // 16) * 16


def stack(scratch, pieces):
    deep = pieces[0].shape[0]
    stride = stride_of(deep)
    for k, piece in enumerate(pieces):
        if stride > deep:
            tail = slice(k * stride + deep // 16 * 16, (k + 1) * stride)
            scratch[tail] = jnp.zeros_like(scratch[tail])
        scratch[k * stride : k * stride + deep] = piece[...]


def pick_rows(pieces, picks, deep, peers):
    width = pieces[0].shape[1]
    tile = tile_of(width, 1024)
    count = len(pieces)
    stride = stride_of(deep)

    def kernel(refs):
        parts, pick, outs = refs[:count], refs[count], refs[count + 1 :]
        for n in range(0, width, tile):
            columns = slice(n, n + tile)
            block = [p[:, columns] for p in parts]
            block = jnp.concatenate(block, 0) if count > 1 else block[0]
            rows = dot(pick[...], block).astype(BF16)
            for k, out in enumerate(outs):
                out[:, columns] = rows[k * stride : k * stride + deep]

    return call(kernel, [*pieces, picks], [jax.ShapeDtypeStruct((deep, width), BF16)] * peers, [])


def weigh_rows(returned, weighing, piece_rows):
    deep, width = returned[0].shape
    tile = tile_of(width, 1024)
    count = len(returned)

    def kernel(refs):
        parts, weigh, outs, laid = refs[:count], refs[count], refs[count + 1 : -1], refs[-1]
        stack(laid, parts)
        for n in range(0, width, tile):
            columns = slice(n, n + tile)
            sums = dot(weigh[...], laid[:, columns]).astype(BF16)
            first = 0
            for out, part in zip(outs, piece_rows):
                out[:, columns] = sums[first : first + part]
                first += part

    return call(
        kernel, [*returned, weighing],
        [jax.ShapeDtypeStruct((part, width), BF16) for part in piece_rows],
        [pltpu.VMEM((count * stride_of(deep), width), BF16)],
    )


def run_expert(arrived, w_up_t, w_down):
    deep, width = arrived[0].shape
    hidden = w_down.shape[0]
    tile = tile_of(width, 1024)
    count = len(arrived)
    stride = stride_of(deep)
    rows = count * stride

    def kernel(refs):
        parts, up, down, outs = refs[:count], refs[count], refs[count + 1], refs[count + 2 : -2]
        laid, activated = refs[-2:]
        stack(laid, parts)
        for first in range(0, hidden, EXPERT_TILE):
            units = slice(first, min(first + EXPERT_TILE, hidden))
            positive = jnp.maximum(
                lax.dot_general(
                    laid[...], up[units], (((1,), (1,)), ((), ())), preferred_element_type=F32
                ),
                0.0,
            )
            activated[:, units] = (positive * positive).astype(BF16)
        for n in range(0, width, tile):
            columns = slice(n, n + tile)
            result = dot(activated[...], down[:, columns]).astype(BF16)
            for k, out in enumerate(outs):
                out[:, columns] = result[k * stride : k * stride + deep]

    return call(
        kernel, [*arrived, w_up_t, w_down], [jax.ShapeDtypeStruct((deep, width), BF16)] * count,
        [pltpu.VMEM((rows, width), BF16), pltpu.VMEM((rows, hidden), BF16)],
    )


def shards(
    tokens,
    mamba_gain,
    w_z,
    w_x,
    w_bc,
    w_dt,
    dt_bias,
    a_log,
    conv_x,
    conv_bc,
    skip,
    norm_gain,
    w_out,
    moe_gain,
    expert_ids,
    router_weights,
    w_up,
    w_down,
):
    wide_count = lax.axis_size("wide")
    ctx_count = lax.axis_size("ctx")
    tok_rows, model_width = tokens.shape
    heads_here = dt_bias.shape[0]
    inner_here = w_z.shape[1]
    head_dim = inner_here // heads_here
    position = lax.axis_index("wide")
    ctx_index = lax.axis_index("ctx")
    ring = Ring(wide_count)
    sizes = [len(group) for group in ring.groups]

    high = router_weights.astype(BF16)
    low = (router_weights - high.astype(F32)).astype(BF16)
    marks = [(expert_ids // LANES).astype(BF16), (expert_ids % LANES).astype(BF16), high, low]
    marks = jnp.pad(jnp.concatenate(marks, 1), ((0, 0), (0, LANES - 4 * TOP)))
    normed = normed_with_marks(tokens, mamba_gain, marks)

    members = wide_count // GROUPS

    def whole_bc(share):
        for bit_number in range(members.bit_length() - 1):
            partner = partner_2(share, "wide", bit_number)
            upper_half = position // 2**bit_number % 2
            share = jnp.where(
                upper_half == 1,
                jnp.concatenate([partner, share], 1),
                jnp.concatenate([share, partner], 1),
            )
        return share

    def per_head(values):
        return jnp.pad(values, (0, LANES - heads_here))[None]

    w_steps = lax.dynamic_slice_in_dim(w_dt, position * heads_here, heads_here, 1)
    w_steps = jnp.pad(w_steps, ((0, 0), (0, LANES - heads_here)))
    group_index = position // members
    taps_bc = lax.dynamic_slice_in_dim(conv_bc, group_index * 2 * STATE, 2 * STATE, 1)
    ssd_params = [per_head(dt_bias), per_head(-jnp.exp(a_log)), conv_x, taps_bc]
    ssd_params += [per_head(skip)]

    devices = ctx_count * wide_count
    capacity = max(2, (7 * tok_rows * TOP + 6 * devices - 1) // (6 * devices))
    deeps = [-(-size * capacity // 8) * 8 for size in sizes]
    peers = (ctx_index ^ jnp.arange(ctx_count, dtype=jnp.int32)) * wide_count + position

    def mix(held, *end):
        gate, x_in, bc_in, steps, marks, *rim = project(held, [w_z, w_x, w_bc, w_steps], *end)
        return [gate, x_in, bc_in, steps, marks, *rim]

    held, projected = [normed], []
    for g in range(ring.half):
        coming = ring.forward(held, g)
        done = mix(held)
        done[2] = whole_bc(done[2])
        held, done, ssd_params = lax.optimization_barrier((coming, done, ssd_params))
        projected.append(done)
    if members > 1:
        done = mix(held)
        done[2] = whole_bc(done[2])
        projected.append(done)
        rim = last_rows(sizes, tok_rows, ring.order, projected)
    else:
        *done, rim = mix(held, ring.order, sizes, projected)
        projected.append(done)
    rim = shifted(rim, "ctx", 1)
    blocks, starts, passed, total = ssd_span(
        sizes, tok_rows, heads_here, ring.order, projected, rim, ssd_params
    )

    prior = jnp.zeros_like(total)
    scans = ctx_count.bit_length() - 1

    for bit_number in range(scans - 1):
        upper = (ctx_index // 2**bit_number % 2)[None]
        other = partner_2(total, "ctx", bit_number)
        prior, total = join_states(upper, total, prior, other, bit_number == scans - 2)
    upper = (ctx_index // 2 ** (scans - 1) % 2)[None]
    other = partner_2(total[:STATE], "ctx", scans - 1)

    piece_rows = ring.pieces(tok_rows)
    gate_params = [norm_gain[None]]

    weights = [w_up[0].T, w_down[0]]
    routing = []

    def share(g, token):
        entering = prior if token is None else after(prior, token)
        parts = gate_and_project(
            ring.spots[g], sizes[g], piece_rows[g], head_dim, ring.order, upper, [*blocks[g], projected[g][0]],
            starts, passed, entering, other, gate_params, w_out, MOST_VMEM if g == ring.half else VMEM_BYTES,
        )
        if g == max(ring.half - 2, 0):
            routing[:] = route(sizes, tok_rows, deeps, peers, after([p[4] for p in projected], token))
            parts, routing[:] = lax.optimization_barrier((parts, routing))
        return parts

    terms = ring.scatter_sum(share, False)
    picks, weighings = routing
    hidden_stream, moe_in = hidden_and_normed(tokens, terms, moe_gain)
    hidden_f32 = hidden_stream.astype(F32)

    def swap(pieces):
        return [
            lax.ppermute(piece, "ctx", [(i, i ^ d) for i in range(ctx_count)]) if d else piece
            for d, piece in enumerate(pieces)
        ]

    held, crossed, expert_outs = [moe_in], None, []
    for g in range(ring.half):
        coming = ring.forward(held, g)
        crossing = swap(pick_rows(held, picks[g], deeps[g], ctx_count))
        done = run_expert(crossed, *weights) if g else None
        held, crossed, done = lax.optimization_barrier((coming, crossing, done))
        expert_outs.append(done)
    crossing = swap(pick_rows(held, picks[-1], deeps[-1], ctx_count))
    done = run_expert(crossed, *weights)
    crossed, done = lax.optimization_barrier((crossing, done))
    expert_outs = expert_outs[1:] + [done, run_expert(crossed, *weights)]

    def result(g, token):
        leaving = expert_outs[g] if token is None else after(expert_outs[g], token)
        return weigh_rows(swap(leaving), weighings[g], piece_rows[g])

    return (hidden_f32 + sum(term.astype(F32) for term in ring.scatter_sum(result, False))).astype(BF16)


def solution(mesh):
    placed = (
        P(("ctx", "wide"), None),
        P(),
        P(None, "wide"),
        P(None, "wide"),
        P(None, "wide"),
        P(),
        P("wide"),
        P("wide"),
        P(None, "wide"),
        P(),
        P("wide"),
        P("wide"),
        P("wide", None),
        P(),
        P(("ctx", "wide"), None),
        P(("ctx", "wide"), None),
        P(("ctx", "wide"), None, None),
        P(("ctx", "wide"), None, None),
    )
    return jax.shard_map(
        shards, mesh=mesh, in_specs=placed, out_specs=P(("ctx", "wide"), None), check_vma=False
    )
```

```python
import jax
import jax.numpy as jnp
from jax import lax
from jax.experimental import pallas as pl
from jax.experimental.pallas import tpu as pltpu
from jax.sharding import PartitionSpec as P

STATE = 128
GROUPS = 8
KERNEL = 4
TOP = 6
RIM = 8

EPSILON = 1e-05
PRECISE = lax.Precision.HIGHEST
LANES = 128
EXPERT_TILE = 512
VMEM_BYTES = 16 * 1024 * 1024
MOST_VMEM = 56 * 1024 * 1024


def ring_of(count):
    columns = 1
    while columns * columns * 4 <= count:
        columns *= 2
    rows = count // columns
    if columns == 1 or rows % 2:
        return list(range(count))
    walk = [row * columns for row in range(rows)]
    for lap, row in enumerate(reversed(range(rows))):
        line = list(range(1, columns))
        if lap % 2:
            line.reverse()
        walk += [row * columns + column for column in line]
    return walk


class Ring:
    def __init__(self, count):
        self.count = count
        self.half = count // 2
        self.walk = ring_of(count)
        place = [0] * count
        for spot, index in enumerate(self.walk):
            place[index] = spot
        following = [(self.walk[i], self.walk[(i + 1) % count]) for i in range(count)]
        self.routes = {1: following, -1: [(b, a) for a, b in following]}
        here = jnp.asarray(place, jnp.int32)[lax.axis_index("wide")]
        self.groups = [[0]] + [[s, -s] for s in range(1, self.half)] + [[self.half]]
        self.spots = [sum(len(group) for group in self.groups[:g]) for g in range(self.half + 1)]
        flat = jnp.asarray([o for group in self.groups for o in group], jnp.int32)
        self.order = jnp.asarray(self.walk, jnp.int32)[(here + flat + count) % count]

    def send(self, block, way):
        return lax.ppermute(block, "wide", self.routes[way])

    def forward(self, held, step, halves=True):
        ahead, behind = held[0], held[-1]
        if step + 1 < self.half:
            return [self.send(ahead, -1), self.send(behind, 1)]
        if not halves:
            return [self.send(behind, 1)]
        cut = ahead.shape[0] // 2
        return [self.send(behind[:cut], 1), self.send(ahead[cut:], -1)]

    def pieces(self, rows):
        return [[rows]] + [[rows, rows]] * (self.half - 1) + [[rows // 2, rows - rows // 2]]

    def scatter_sum(self, part, add):
        far = part(self.half, None)
        up, down = self.send(far[0], 1), self.send(far[1], -1)
        following = part(self.half - 1, far[0])
        for s in range(self.half - 1, 0, -1):
            ahead, behind = add(following, [up, down])
            up, down = self.send(ahead, 1), self.send(behind, -1)
            following = part(s - 1, ahead)
        return [following[0], up, down]


def after(values, *others):
    return lax.optimization_barrier((values, others))[0]


def partner_2(block, axis, bit):
    count = lax.axis_size(axis)
    route = []
    for low in range(count):
        high = low | 1 << bit
        if high != low and high < count:
            route += [(low, high), (high, low)]
    return lax.ppermute(block, axis, route)


def shifted(block, axis, distance):
    devices = range(lax.axis_size(axis))
    route = [(i - distance, i) for i in devices if i - distance in devices]
    return lax.ppermute(block, axis, route)


def fan_of(heads, head_dim):
    head_id = lax.broadcasted_iota(jnp.int32, (LANES, heads * head_dim), 0)
    first = head_id * head_dim
    unit_id = lax.broadcasted_iota(jnp.int32, (LANES, heads * head_dim), 1)
    return jnp.where((unit_id >= first) & (unit_id < first + head_dim), 1.0, 0.0).astype(BF16)


def spread(values, fan):
    high = values.astype(jnp.bfloat16)
    low = (values - high.astype(jnp.float32)).astype(jnp.bfloat16)
    return jnp.dot(high, fan, preferred_element_type=jnp.float32) + jnp.dot(
        low, fan, preferred_element_type=jnp.float32
    )


def softplus(values):
    return jnp.maximum(values, 0.0) + jnp.log1p(jnp.exp(-jnp.abs(values)))


def silu(values):
    return values / (1.0 + jnp.exp(-values))


def conv_silu(current, before, taps):
    rows = current.shape[0]
    extended = jnp.concatenate([before, current], 0)
    first = RIM - (KERNEL - 1)
    total = taps[0:1] * extended[first : first + rows]
    for offset in range(1, KERNEL):
        total = total + taps[offset : offset + 1] * extended[first + offset : first + offset + rows]
    return silu(total)


def tile_of(width, limit):
    parts = width // LANES
    return LANES * max(k for k in range(1, parts + 1) if parts % k == 0 and k * LANES <= limit)


class Late:
    def __init__(self, source, target, arrival):
        self.target = target
        self.copy = pltpu.make_async_copy(source, target, arrival)
        self.copy.start()
        self.waiting = True

    def __call__(self):
        if self.waiting:
            self.copy.wait()
            self.waiting = False
        return self.target


def call(kernel, ins, outs, scratch, scalars=0, late=0, away=0, room=None):
    def body(*refs):
        refs = list(refs)
        if late:
            arrivals = refs.pop()
            for k in range(late):
                refs[scalars + k] = Late(refs[scalars + k], refs[k - late], arrivals.at[k])
            refs = refs[:-late]
        kernel(refs)

    coming = ins[scalars : scalars + late]
    extra = [pltpu.VMEM(a.shape, a.dtype) for a in coming]
    extra += [pltpu.SemaphoreType.DMA((late,))] if late else []
    return pl.pallas_call(
        body,
        out_shape=outs,
        in_specs=[pl.BlockSpec(memory_space=pltpu.SMEM)] * scalars
        + [pl.BlockSpec(memory_space=pl.ANY)] * late
        + [pl.BlockSpec(memory_space=pltpu.VMEM)] * (len(ins) - scalars - late),
        out_specs=[pl.BlockSpec(memory_space=pl.ANY)] * away
        + [pl.BlockSpec(memory_space=pltpu.VMEM)] * (len(outs) - away),
        scratch_shapes=list(scratch) + extra,
        compiler_params=pltpu.CompilerParams(vmem_limit_bytes=room or VMEM_BYTES),
        cost_estimate=BRIEF,
    )(*ins)


BRIEF = pl.CostEstimate(flops=1, bytes_accessed=1, transcendentals=0)
BF16, F32 = jnp.bfloat16, jnp.float32


def dot(a, b):
    return jnp.dot(a, b, preferred_element_type=F32)


def normed_with_marks(tokens, gain, marks):
    rows, width = tokens.shape

    def kernel(refs):
        tokens, gain, marks, out = refs
        values = tokens[...].astype(F32)
        mean_sq = jnp.sum(values * values, axis=1, keepdims=True) / width
        out[:, :width] = (values * lax.rsqrt(mean_sq + EPSILON) * gain[...]).astype(BF16)
        out[:, width:] = marks[...]

    outs = [jax.ShapeDtypeStruct((rows, width + LANES), BF16)]
    return call(kernel, [tokens, gain[None], marks], outs, [])[0]


def project(pieces, weights, order=None, sizes=(), earlier=()):
    rows = sum(p.shape[0] for p in pieces)
    depth = weights[0].shape[0]
    count, outs = len(pieces), len(weights)
    count_all = sum(sizes)
    block_rows = rows // sizes[-1] if sizes else 0
    scalars = [order] if sizes else []
    far = [p[k] for k in (1, 2) for p in earlier]
    ins = [*scalars, *far, *pieces, *weights]

    def kernel(*refs):
        order, refs = (refs[0], refs[1:]) if sizes else (None, refs)
        edges, refs = refs[: len(far)], refs[len(far) :]
        parts, weight_refs = refs[:count], refs[count : count + outs]
        out_refs = refs[count + outs : count + 2 * outs + 1]
        if sizes:
            rim, x_edge, bc_edge, arrivals = refs[count + 2 * outs + 1 :]
            spot = 0
            for g, size in enumerate(sizes[:-1]):
                for j in range(size):
                    edge = pl.ds((j + 1) * block_rows - 2 * RIM, 2 * RIM)

                    @pl.when(order[spot] == count_all - 1)
                    def _(g=g, edge=edge):
                        copies = [
                            pltpu.make_async_copy(edges[g].at[edge], x_edge, arrivals.at[0]),
                            pltpu.make_async_copy(edges[len(earlier) + g].at[edge], bc_edge, arrivals.at[1]),
                        ]
                        for copy in copies:
                            copy.start()
                        for copy in copies:
                            copy.wait()

                    spot += 1
        block = [p[:, :depth] for p in parts]
        block = jnp.concatenate(block, 0) if count > 1 else block[0]
        for weight, out in zip(weight_refs, out_refs):
            out[...] = dot(block, weight[...]).astype(out.dtype)
        first = 0
        for p in parts:
            out_refs[-1][first : first + p.shape[0]] = p[:, depth:]
            first += p.shape[0]
        if sizes:

            @pl.when(order[spot] == count_all - 1)
            def _():
                x_edge[...] = out_refs[1][rows - 2 * RIM :]
                bc_edge[...] = out_refs[2][rows - 2 * RIM :]

            rim[:, : x_edge.shape[1]] = x_edge[...].astype(F32)[RIM:]
            rim[:, x_edge.shape[1] :] = bc_edge[...].astype(F32)[RIM:]

    shape = jax.ShapeDtypeStruct
    widths = [w.shape[1] for w in weights]
    shapes = [shape((rows, width), BF16) for width in widths[:-1]]
    shapes += [shape((rows, widths[-1]), F32), shape((rows, LANES), BF16)]
    scratch = []
    if sizes:
        shapes.append(shape((RIM, widths[1] + widths[2]), F32))
        scratch = [
            pltpu.VMEM((2 * RIM, widths[1]), BF16),
            pltpu.VMEM((2 * RIM, widths[2]), BF16),
            pltpu.SemaphoreType.DMA((2,)),
        ]
    return pl.pallas_call(
        kernel,
        grid=(1,),
        out_shape=shapes,
        in_specs=[pl.BlockSpec(memory_space=pltpu.SMEM)] * len(scalars)
        + [pl.BlockSpec(memory_space=pl.ANY)] * len(far)
        + [pl.BlockSpec(memory_space=pltpu.VMEM)] * (count + outs),
        out_specs=[pl.BlockSpec(a.shape, lambda i: (0, 0)) for a in shapes],
        scratch_shapes=scratch,
        compiler_params=pltpu.CompilerParams(vmem_limit_bytes=VMEM_BYTES),
        cost_estimate=BRIEF,
    )(*ins)


def add_terms(own, arrived):
    def kernel(refs):
        ahead, behind, up, down, ahead_out, behind_out = refs
        for term, other, out, last in ((ahead, up, ahead_out, False), (behind, down, behind_out, True)):
            rows, cut = term.shape[0], other.shape[0]
            span = slice(rows - cut, rows) if last else slice(0, cut)
            out[span] = (term[span].astype(F32) + other[...].astype(F32)).astype(out.dtype)
            if cut < rows:
                rest = slice(0, rows - cut) if last else slice(cut, rows)
                out[rest] = term[rest]

    outs = [jax.ShapeDtypeStruct(p.shape, p.dtype) for p in own]
    return call(kernel, [*own, *arrived], outs, [])


def hidden_and_normed(tokens, terms, gain):
    def kernel(refs):
        tokens, own, up, down, gain, hidden_out, normed_out = refs
        total = own[...].astype(F32) + up[...].astype(F32) + down[...].astype(F32)
        hidden = (tokens[...].astype(F32) + total).astype(BF16)
        hidden_out[...] = hidden
        hidden = hidden.astype(F32)
        mean_sq = jnp.sum(hidden * hidden, axis=1, keepdims=True) / tokens.shape[1]
        normed_out[...] = (hidden * lax.rsqrt(mean_sq + EPSILON) * gain[...]).astype(BF16)

    outs = [jax.ShapeDtypeStruct(tokens.shape, BF16)] * 2
    return call(kernel, [tokens, *terms, gain[None]], outs, [])


def last_rows(sizes, rows, order, projected):
    found = 0.0
    spot = 0
    for g, size in enumerate(sizes):
        for j in range(size):
            edge = slice((j + 1) * rows - RIM, (j + 1) * rows)
            both = jnp.concatenate([projected[g][1][edge], projected[g][2][edge]], 1).astype(F32)
            found = found + jnp.where(order[spot] == sum(sizes) - 1, both, 0.0)
            spot += 1
    return found


def join_states(upper, total, prior, other, last):
    def join(earlier, later):
        state = jnp.exp(later[STATE : STATE + 1]) * earlier[:STATE] + later[:STATE]
        return state, earlier[STATE:] + later[STATE:]

    def kernel(refs):
        upper, total, prior, other, prior_out, total_out = refs

        def put(ref, value):
            ref[:STATE] = value[0].astype(ref.dtype)
            if ref.shape[0] > STATE:
                ref[STATE:] = value[1]

        @pl.when(upper[0] == 1)
        def _():
            put(prior_out, join(other, prior))
            put(total_out, join(other, total))

        @pl.when(upper[0] == 0)
        def _():
            prior_out[...] = prior[...]
            put(total_out, join(total, other))

    shape = jax.ShapeDtypeStruct
    outs = [shape(total.shape, F32)]
    outs += [shape((STATE, total.shape[1]), BF16) if last else shape(total.shape, F32)]
    return call(kernel, [upper, total, prior, other], outs, [], 1)


def ssd_span(sizes, rows, heads, order, projected, rim, params):
    pieces = len(sizes)
    count = sum(sizes)
    width = projected[0][1].shape[1]
    head_dim = width // heads
    ins = [order, *(p[k] for k in (1, 2, 3) for p in projected[:-1])]
    ins += [projected[-1][k] for k in (1, 2, 3)] + [rim, *params]

    def kernel(refs):
        order = refs[0]
        before = pieces - 1
        x_in, bc_in, steps = (
            [*refs[1 + k * before : 1 + (k + 1) * before], refs[1 + 3 * before + k]] for k in range(3)
        )
        rim, bias, rate, taps_x, taps_bc, skip_heads = refs[1 + 3 * pieces : 7 + 3 * pieces]
        refs = refs[7 + 3 * pieces :]
        fan = fan_of(heads, head_dim)
        skip_row = spread(jnp.broadcast_to(skip_heads[...], (8, LANES)), fan)[0:1]
        x_in, bc_in, steps = ([*arrays[:-1], lambda last=arrays[-1]: last] for arrays in (x_in, bc_in, steps))
        y_out, c_out, cum_out = (refs[k * pieces : (k + 1) * pieces] for k in range(3))
        starts_out, passed_out, total_out, tails_x, tails_bc, grown, lasts = refs[3 * pieces : 3 * pieces + 7]
        y_all, c_all, cum_all, starts, passed_all, leaving = refs[3 * pieces + 7 :]
        copies = []

        def take_away(source, target):
            copies.append(pltpu.make_async_copy(source, target, leaving.at[len(copies)]))
            copies[-1].start()

        row_id = lax.broadcasted_iota(jnp.int32, (rows, rows), 0)
        col_id = lax.broadcasted_iota(jnp.int32, (rows, rows), 1)
        causal = row_id >= col_id
        lower = jnp.where(causal, 1.0, 0.0).astype(F32)
        pair = 2 * head_dim
        left = lax.broadcasted_iota(jnp.int32, (rows, pair), 1) < head_dim
        spots = [(g, j) for g, size in enumerate(sizes) for j in range(size)]
        tails_x[0] = rim[:, :width]
        tails_bc[0] = rim[:, width:]
        for spot, (g, j) in enumerate(spots):
            edge = slice((j + 1) * rows - 2 * RIM, (j + 1) * rows)
            tails_x[order[spot] + 1] = x_in[g]()[edge].astype(F32)[RIM:]
            tails_bc[order[spot] + 1] = bc_in[g]()[edge].astype(F32)[RIM:]
        for spot, (g, j) in enumerate(spots):
            span = slice(j * rows, (j + 1) * rows)
            seq = order[spot]
            x = conv_silu(x_in[g]()[span].astype(F32), tails_x[seq], taps_x[...])
            bc = conv_silu(bc_in[g]()[span].astype(F32), tails_bc[seq], taps_bc[...])
            c = bc[:, STATE:].astype(BF16)
            b_t = jnp.transpose(bc[:, :STATE]).astype(BF16)
            dt = softplus(steps[g]()[span] + bias[...])
            cum = jnp.dot(lower, dt * rate[...], precision=PRECISE, preferred_element_type=F32)
            cum_t = jnp.transpose(cum)
            last = cum[rows - 1 : rows]
            scores = dot(c, b_t)
            x_dt = x * spread(dt, fan)
            x_low = x_dt.astype(BF16)
            direct = skip_row * x
            for h in range(0, heads, 2):
                weights = []
                for k in (h, h + 1):
                    gap = cum[:, k : k + 1] - cum_t[k : k + 1, :]
                    weights.append((scores * jnp.exp(jnp.where(causal, gap, -1e30))).astype(BF16))
                units = slice(h * head_dim, h * head_dim + pair)
                both = x_low[:, units]
                none = jnp.zeros_like(both)
                stacked = jnp.concatenate([jnp.where(left, both, none), jnp.where(left, none, both)], 0)
                y_all[spot, :, units] = dot(jnp.concatenate(weights, 1), stacked) + direct[:, units]
            tail = (x_dt * spread(jnp.exp(last - cum), fan)).astype(BF16)
            grown[seq] = dot(b_t, tail)
            lasts[seq] = jnp.broadcast_to(last, (8, LANES))
            c_all[spot] = c
            cum_all[spot] = cum
            away = pl.ds(j * rows, rows)
            take_away(y_all.at[spot], y_out[g].at[away])
            take_away(c_all.at[spot], c_out[g].at[away])
            take_away(cum_all.at[spot], cum_out[g].at[away])
        state = jnp.zeros((STATE, width), F32)
        passed = jnp.zeros((8, LANES), F32)
        for i in range(count):
            last = lasts[i]
            starts[i] = state.astype(BF16)
            passed_all[i] = passed
            state = spread(jnp.exp(last), fan)[0:1] * state + grown[i]
            passed = passed + last
        take_away(starts, starts_out)
        take_away(passed_all, passed_out)
        total_out[:STATE] = state
        total_out[STATE:] = spread(passed, fan)
        for copy in copies:
            copy.wait()

    shape = jax.ShapeDtypeStruct
    outs = [shape((size * rows, width), F32) for size in sizes]
    outs += [shape((size * rows, STATE), BF16) for size in sizes]
    outs += [shape((size * rows, LANES), F32) for size in sizes]
    outs += [shape((count, STATE, width), BF16), shape((count, 8, LANES), F32)]
    outs += [shape((STATE + 8, width), F32)]
    scratch = [
        pltpu.VMEM((count + 1, RIM, width), F32),
        pltpu.VMEM((count + 1, RIM, 2 * STATE), F32),
        pltpu.VMEM((count, STATE, width), F32),
        pltpu.VMEM((count, 8, LANES), F32),
        pltpu.VMEM((count, rows, width), F32),
        pltpu.VMEM((count, rows, STATE), BF16),
        pltpu.VMEM((count, rows, LANES), F32),
        pltpu.VMEM((count, STATE, width), BF16),
        pltpu.VMEM((count, 8, LANES), F32),
        pltpu.SemaphoreType.DMA((3 * count + 2,)),
    ]
    done = call(kernel, ins, outs, scratch, 1, 3 * (pieces - 1), 3 * pieces + 2, MOST_VMEM)
    return list(zip(done[:pieces], done[pieces:], done[2 * pieces :])), *done[3 * pieces :]


def route(sizes, rows, deeps, peers, marks):
    count = peers.shape[0]

    def kernel(refs):
        peers, marks = refs[0], refs[1 : 1 + len(sizes)]
        picks, weighings = refs[1 + len(sizes) : 1 + 2 * len(sizes)], refs[1 + 2 * len(sizes) :]
        for g, size in enumerate(sizes):
            stride = stride_of(deeps[g])
            slots = count * stride
            tokens = size * rows
            part = marks[g][...].astype(F32)
            columns = [part[:, k * TOP : (k + 1) * TOP] for k in range(4)]
            ids, shares = columns[0] * LANES + columns[1], columns[2] + columns[3]
            lane = lax.broadcasted_iota(jnp.int32, (tokens, LANES), 1)
            member = jnp.zeros((tokens, LANES), F32)
            weight = jnp.zeros((tokens, LANES), F32)
            for p in range(count):
                named = ids == peers[p].astype(F32)
                here = jnp.max(jnp.where(named, 1.0, 0.0), axis=1, keepdims=True)
                share = jnp.sum(jnp.where(named, shares, 0.0), axis=1, keepdims=True)
                member = jnp.where(lane == p, here, member)
                weight = jnp.where(lane == p, share, weight)
            row_id = lax.broadcasted_iota(jnp.int32, (tokens, tokens), 0)
            col_id = lax.broadcasted_iota(jnp.int32, (tokens, tokens), 1)
            earlier = jnp.where(row_id > col_id, 1.0, 0.0).astype(BF16)
            rank = jnp.where(member > 0.0, dot(earlier, member.astype(BF16)), -1.0)
            peer_id = lax.broadcasted_iota(jnp.int32, (LANES, slots), 0)
            slot_id = lax.broadcasted_iota(jnp.int32, (LANES, slots), 1)
            first = peer_id * stride
            fan = jnp.where((slot_id >= first) & (slot_id < first + stride), 1.0, 0.0).astype(BF16)
            wanted = lax.rem(lax.broadcasted_iota(jnp.int32, (tokens, slots), 1), stride).astype(F32)
            found = dot(rank.astype(BF16), fan) == wanted
            weighings[g][...] = jnp.where(found, dot(weight.astype(BF16), fan), 0.0).astype(BF16)
            picks[g][...] = jnp.transpose(jnp.where(found, 1.0, 0.0)).astype(BF16)

    shape = jax.ShapeDtypeStruct
    widths = [count * stride_of(deep) for deep in deeps]
    outs = [shape((width, size * rows), BF16) for width, size in zip(widths, sizes)]
    outs += [shape((size * rows, width), BF16) for width, size in zip(widths, sizes)]
    done = call(kernel, [peers, *marks], outs, [], 1)
    return done[: len(sizes)], done[len(sizes) :]


def gate_and_project(spot, size, piece_rows, head_dim, order, upper, blocks, starts, passed, prior, other, params, w_out, room):
    rows = sum(piece_rows) // size
    ins = [order, upper, *blocks, starts, passed, w_out, prior, other, *params]

    def kernel(refs):
        (order, upper, y_ref, c_ref, cum_ref, gate_ref, starts, passed, w_ref, prior, other, gain) = refs[:12]
        outs, gated_all = refs[12:-1], refs[-1]
        fan = fan_of(w_out.shape[0] // head_dim, head_dim)
        arrived = jnp.exp(prior[STATE : STATE + 1]) * other[...].astype(F32)
        incoming = prior[:STATE] + jnp.where(upper[0] == 1, arrived, 0.0)
        for j in range(size):
            seq = order[spot + j]
            span = slice(j * rows, (j + 1) * rows)
            fade = spread(jnp.exp(passed()[seq]), fan)[0:1]
            state = starts()[seq].astype(F32) + fade * incoming
            earlier = dot(c_ref()[span], state.astype(BF16))
            y = y_ref()[span] + spread(jnp.exp(cum_ref()[span]), fan) * earlier
            gated = y * silu(gate_ref()[span].astype(F32))
            squares = lax.dot_general(
                (gated * gated).astype(BF16), fan, (((1,), (1,)), ((), ())), preferred_element_type=F32
            )
            scale = lax.rsqrt(squares / head_dim + EPSILON)
            gated_all[span] = (gated * spread(scale, fan) * gain[...]).astype(BF16)
        w_ref = w_ref()
        tile = tile_of(w_ref.shape[1], 1024)
        for n in range(0, w_ref.shape[1], tile):
            columns = slice(n, n + tile)
            share = dot(gated_all[...], w_ref[:, columns]).astype(BF16)
            first = 0
            for out, part in zip(outs, piece_rows):
                out[:, columns] = share[first : first + part]
                first += part

    outs = [jax.ShapeDtypeStruct((part, w_out.shape[1]), BF16) for part in piece_rows]
    return call(kernel, ins, outs, [pltpu.VMEM((size * rows, w_out.shape[0]), BF16)], 2, 7, 0, room)


def stride_of(deep):
    return -(-deep // 16) * 16


def stack(scratch, pieces):
    deep = pieces[0].shape[0]
    stride = stride_of(deep)
    for k, piece in enumerate(pieces):
        if stride > deep:
            tail = slice(k * stride + deep // 16 * 16, (k + 1) * stride)
            scratch[tail] = jnp.zeros_like(scratch[tail])
        scratch[k * stride : k * stride + deep] = piece[...]


def pick_rows(pieces, picks, deep, peers):
    width = pieces[0].shape[1]
    tile = tile_of(width, 1024)
    count = len(pieces)
    stride = stride_of(deep)

    def kernel(refs):
        parts, pick, outs = refs[:count], refs[count], refs[count + 1 :]
        for n in range(0, width, tile):
            columns = slice(n, n + tile)
            block = [p[:, columns] for p in parts]
            block = jnp.concatenate(block, 0) if count > 1 else block[0]
            rows = dot(pick[...], block).astype(BF16)
            for k, out in enumerate(outs):
                out[:, columns] = rows[k * stride : k * stride + deep]

    return call(kernel, [*pieces, picks], [jax.ShapeDtypeStruct((deep, width), BF16)] * peers, [])


def weigh_rows(returned, weighing, piece_rows, arrived=()):
    deep, width = returned[0].shape
    tile = tile_of(width, 1024)
    count = len(returned)
    others = len(arrived)

    def kernel(refs):
        parts, weigh, added = refs[:count], refs[count], refs[count + 1 : count + 1 + others]
        outs, laid = refs[count + 1 + others : -1], refs[-1]
        stack(laid, parts)
        for n in range(0, width, tile):
            columns = slice(n, n + tile)
            sums = dot(weigh[...], laid[:, columns])
            first = 0
            for k, (out, part) in enumerate(zip(outs, piece_rows)):
                term = sums[first : first + part]
                first += part
                if others:
                    cut = added[k].shape[0]
                    near = slice(part - cut, part) if k else slice(0, cut)
                    rest = slice(0, part - cut) if k else slice(cut, part)
                    out[near, columns] = (term[near] + added[k][:, columns].astype(F32)).astype(BF16)
                    if cut < part:
                        out[rest, columns] = term[rest].astype(BF16)
                else:
                    out[:, columns] = term.astype(BF16)

    return call(
        kernel, [*returned, weighing, *arrived],
        [jax.ShapeDtypeStruct((part, width), BF16) for part in piece_rows],
        [pltpu.VMEM((count * stride_of(deep), width), BF16)],
    )


def run_expert(arrived, w_up_t, w_down):
    deep, width = arrived[0].shape
    hidden = w_down.shape[0]
    tile = tile_of(width, 1024)
    count = len(arrived)
    stride = stride_of(deep)
    rows = count * stride

    def kernel(refs):
        parts, up, down, outs = refs[:count], refs[count], refs[count + 1], refs[count + 2 : -2]
        laid, activated = refs[-2:]
        stack(laid, parts)
        for first in range(0, hidden, EXPERT_TILE):
            units = slice(first, min(first + EXPERT_TILE, hidden))
            positive = jnp.maximum(
                lax.dot_general(
                    laid[...], up[units], (((1,), (1,)), ((), ())), preferred_element_type=F32
                ),
                0.0,
            )
            activated[:, units] = (positive * positive).astype(BF16)
        for n in range(0, width, tile):
            columns = slice(n, n + tile)
            result = dot(activated[...], down[:, columns]).astype(BF16)
            for k, out in enumerate(outs):
                out[:, columns] = result[k * stride : k * stride + deep]

    return call(
        kernel, [*arrived, w_up_t, w_down], [jax.ShapeDtypeStruct((deep, width), BF16)] * count,
        [pltpu.VMEM((rows, width), BF16), pltpu.VMEM((rows, hidden), BF16)],
    )


def shards(
    tokens,
    mamba_gain,
    w_z,
    w_x,
    w_bc,
    w_dt,
    dt_bias,
    a_log,
    conv_x,
    conv_bc,
    skip,
    norm_gain,
    w_out,
    moe_gain,
    expert_ids,
    router_weights,
    w_up,
    w_down,
):
    wide_count = lax.axis_size("wide")
    ctx_count = lax.axis_size("ctx")
    tok_rows, model_width = tokens.shape
    heads_here = dt_bias.shape[0]
    inner_here = w_z.shape[1]
    head_dim = inner_here // heads_here
    position = lax.axis_index("wide")
    ctx_index = lax.axis_index("ctx")
    ring = Ring(wide_count)
    sizes = [len(group) for group in ring.groups]

    high = router_weights.astype(BF16)
    low = (router_weights - high.astype(F32)).astype(BF16)
    marks = [(expert_ids // LANES).astype(BF16), (expert_ids % LANES).astype(BF16), high, low]
    marks = jnp.pad(jnp.concatenate(marks, 1), ((0, 0), (0, LANES - 4 * TOP)))
    normed = normed_with_marks(tokens, mamba_gain, marks)

    members = wide_count // GROUPS

    def whole_bc(share):
        for bit_number in range(members.bit_length() - 1):
            partner = partner_2(share, "wide", bit_number)
            upper_half = position // 2**bit_number % 2
            share = jnp.where(
                upper_half == 1,
                jnp.concatenate([partner, share], 1),
                jnp.concatenate([share, partner], 1),
            )
        return share

    def per_head(values):
        return jnp.pad(values, (0, LANES - heads_here))[None]

    w_steps = lax.dynamic_slice_in_dim(w_dt, position * heads_here, heads_here, 1)
    w_steps = jnp.pad(w_steps, ((0, 0), (0, LANES - heads_here)))
    group_index = position // members
    taps_bc = lax.dynamic_slice_in_dim(conv_bc, group_index * 2 * STATE, 2 * STATE, 1)
    ssd_params = [per_head(dt_bias), per_head(-jnp.exp(a_log)), conv_x, taps_bc]
    ssd_params += [per_head(skip)]

    devices = ctx_count * wide_count
    capacity = max(2, (7 * tok_rows * TOP + 6 * devices - 1) // (6 * devices))
    deeps = [-(-size * capacity // 8) * 8 for size in sizes]
    peers = (ctx_index ^ jnp.arange(ctx_count, dtype=jnp.int32)) * wide_count + position

    def mix(held, *end):
        gate, x_in, bc_in, steps, marks, *rim = project(held, [w_z, w_x, w_bc, w_steps], *end)
        return [gate, x_in, bc_in, steps, marks, *rim]

    held, projected = [normed], []
    for g in range(ring.half):
        coming = ring.forward(held, g)
        done = mix(held)
        done[2] = whole_bc(done[2])
        held, done, ssd_params = lax.optimization_barrier((coming, done, ssd_params))
        projected.append(done)
    if members > 1:
        done = mix(held)
        done[2] = whole_bc(done[2])
        projected.append(done)
        rim = last_rows(sizes, tok_rows, ring.order, projected)
    else:
        *done, rim = mix(held, ring.order, sizes, projected)
        projected.append(done)
    rim = shifted(rim, "ctx", 1)
    blocks, starts, passed, total = ssd_span(
        sizes, tok_rows, heads_here, ring.order, projected, rim, ssd_params
    )

    prior = jnp.zeros_like(total)
    scans = ctx_count.bit_length() - 1

    for bit_number in range(scans - 1):
        upper = (ctx_index // 2**bit_number % 2)[None]
        other = partner_2(total, "ctx", bit_number)
        prior, total = join_states(upper, total, prior, other, bit_number == scans - 2)
    upper = (ctx_index // 2 ** (scans - 1) % 2)[None]
    other = partner_2(total[:STATE], "ctx", scans - 1)

    piece_rows = ring.pieces(tok_rows)
    gate_params = [norm_gain[None]]

    weights = [w_up[0].T, w_down[0]]
    routing = []

    def share(g, token):
        entering = prior if token is None else after(prior, token)
        parts = gate_and_project(
            ring.spots[g], sizes[g], piece_rows[g], head_dim, ring.order, upper, [*blocks[g], projected[g][0]],
            starts, passed, entering, other, gate_params, w_out, MOST_VMEM if g == ring.half else VMEM_BYTES,
        )
        if g == max(ring.half - 2, 0):
            routing[:] = route(sizes, tok_rows, deeps, peers, after([p[4] for p in projected], token))
            parts, routing[:] = lax.optimization_barrier((parts, routing))
        return parts

    terms = ring.scatter_sum(share, add_terms)
    picks, weighings = routing
    hidden_stream, moe_in = hidden_and_normed(tokens, terms, moe_gain)
    hidden_f32 = hidden_stream.astype(F32)

    def cross(piece, d):
        return lax.ppermute(piece, "ctx", [(i, i ^ d) for i in range(ctx_count)]) if d else piece

    def swap(pieces):
        return [cross(piece, d) for d, piece in enumerate(pieces)]

    held, crossed, expert_outs = [moe_in], None, []
    for g in range(ring.half):
        coming = ring.forward(held, g)
        crossing = swap(pick_rows(held, picks[g], deeps[g], ctx_count))
        done = run_expert(crossed, *weights) if g else None
        held, crossed, done = lax.optimization_barrier((coming, crossing, done))
        expert_outs.append(done)
    crossing = swap(pick_rows(held, picks[-1], deeps[-1], ctx_count))
    done = run_expert(crossed, *weights)
    crossed, done = lax.optimization_barrier((crossing, done))
    early = [cross(piece, d) for d, piece in enumerate(done) if d <= ctx_count // 2]
    last, early = lax.optimization_barrier((run_expert(crossed, *weights), early))
    expert_outs = expert_outs[1:] + [done, last]

    def result(g, token):
        leaving = expert_outs[g] if token is None else after(expert_outs[g], token)
        back = swap(leaving)
        if g == ring.half - 1:
            back = early + back[len(early) :]
        if 0 < g < ring.half:
            return lambda arrived: weigh_rows(back, weighings[g], piece_rows[g], arrived)
        return weigh_rows(back, weighings[g], piece_rows[g])

    terms = ring.scatter_sum(result, lambda weigh, arrived: weigh(arrived))
    return (hidden_f32 + sum(term.astype(F32) for term in terms)).astype(BF16)


def solution(mesh):
    placed = (
        P(("ctx", "wide"), None),
        P(),
        P(None, "wide"),
        P(None, "wide"),
        P(None, "wide"),
        P(),
        P("wide"),
        P("wide"),
        P(None, "wide"),
        P(),
        P("wide"),
        P("wide"),
        P("wide", None),
        P(),
        P(("ctx", "wide"), None),
        P(("ctx", "wide"), None),
        P(("ctx", "wide"), None, None),
        P(("ctx", "wide"), None, None),
    )
    return jax.shard_map(
        shards, mesh=mesh, in_specs=placed, out_specs=P(("ctx", "wide"), None), check_vma=False
    )
```
